256 devices in a mesh: ctx: 32 (over x, z), hx: 8 (over y, core).
Axes of the slice: x: 4, y: 4, z: 8, core: 2. Of those that a mesh axis runs over, the one named last changes fastest.
Arguments:
- query_latent: bfloat16 [16, 128, 512], P(None, 'hx'), may hold values from -2 to 2
- query_rope: bfloat16 [16, 8192], P(None, 'hx'), may hold values from -80 to 80
- cache_latent: bfloat16 [4, 131072, 512], P(None, ('ctx', 'hx')), may hold values from -16 to 16
- cache_rope: bfloat16 [4, 64, 131072], P(None, None, ('ctx', 'hx')), may hold values from -8 to 8
- suffix_latent: bfloat16 [16, 32768, 512], P(None, ('ctx', 'hx')), may hold values from -16 to 16
- suffix_rope: bfloat16 [16, 64, 32768], P(None, None, ('ctx', 'hx')), may hold values from -6 to 6
- lengths: int32 [4], replicated, may hold values from 32768 to 131072, as said below
- parents: int32 [16], replicated, may hold values from 0 to 15, as said below
- w_uv: bfloat16 [512, 16384], P(None, ('ctx', 'hx')), may hold values from -1.25 to 1.25
- w_o: bfloat16 [16384, 7168], P(('ctx', 'hx')), may hold values from -0.046875 to 0.046875
- hidden: bfloat16 [16, 7168], replicated, may hold values from -6 to 6
- norm_gain: float32 [7168], replicated, may hold values from 0.1 to 1.9
- w_gate: bfloat16 [32768, 7168], P(('ctx', 'hx')), may hold values from -0.0625 to 0.0625
- w_up: bfloat16 [32768, 7168], P(('ctx', 'hx')), may hold values from -0.0625 to 0.0625
- w_down: bfloat16 [32768, 7168], P(('ctx', 'hx')), may hold values from -0.5 to 0.5
- expert_ids: int32 [16, 8], replicated, may hold values from 0 to 15, all different within a row
- gate_weights: float32 [16, 8], replicated, may hold values from 0.1 to 0.6
Outputs:
- attended: bfloat16 [16, 7168], replicated
- updated: bfloat16 [16, 7168], P(None, ('ctx', 'hx'))
The draws below stay inside these ranges and needn't reach their ends.
Inputs may be any that keep to these rules, and one draw needn't show every extreme that they name: `lengths`: one request has length 131072 and another 131072 // 4. parents[b] is a hypothesis of the same request as b. `expert_ids`: each row names 8 different experts.
All inputs are finite; a program needn't handle non-finite values.
Results may differ from the reference program's by a relative error of at most 0.012.
Values may be sent and summed in bfloat16 or wider, within the bound.
A program may use at most 64 MiB of HBM per device.

```python
import math
import jax
import jax.numpy as jnp
from jax import lax

H = 128
DL = 512
DR = 64
DN = 128
DV = 128
D = 7168
EFF = 2048
TOP = 8
EXPERTS = 16
REQ = 4
BEAMS = 4
CTX_DEV = 512
SUF_DEV = 128
HYPS = 16
CTX = 131072
SUF = 32768
DEVICES = 256


def draw_cache_rope(key, part):
    key = jax.random.fold_in(key, 11)
    return jax.random.normal(key, (REQ, DR, CTX), jnp.float32).astype(jnp.bfloat16)


def draw_query_rope(key, part):
    key = jax.random.fold_in(key, 12)
    return jax.random.normal(key, (HYPS, H * DR), jnp.float32).astype(jnp.bfloat16)


def draw_query_latent(key, part):
    key = jax.random.fold_in(key, 13)
    return (0.18 * jax.random.normal(key, (HYPS, H, DL), jnp.float32)).astype(jnp.bfloat16)


def draw_lengths(key, part):
    key = jax.random.fold_in(key, 14)
    key_list = jax.random.split(key, 2)
    ranking = jax.random.permutation(key_list[0], REQ)
    middle = jax.random.randint(key_list[1], (REQ,), CTX // 4, CTX + 1)
    return jnp.where(ranking == 0, CTX, jnp.where(ranking == 1, CTX // 4, middle)).astype(jnp.int32)


def draw_parents(key, part):
    key = jax.random.fold_in(key, 15)
    key_list = jax.random.split(key, 2)
    offsets = jax.random.randint(key_list[0], (REQ, BEAMS), 0, BEAMS)
    slot_rank = jax.vmap(lambda single: jax.random.permutation(single, BEAMS))(jax.random.split(key_list[1], REQ))
    offsets = jnp.where(slot_rank == 0, 0, jnp.where(slot_rank == 1, BEAMS - 1, offsets))
    return (jnp.arange(REQ)[:, None] * BEAMS + offsets).reshape(HYPS).astype(jnp.int32)


def with_spikes(drawn, rng, source, target, shards_of, factor):
    owner, partner = [(jnp.arange(drawn.shape[dim]) // (drawn.shape[dim] // shards_of)).reshape([-1 if axis == dim else 1 for axis in range(drawn.ndim)]) for dim in (source, target)]
    chosen = jax.random.permutation(rng, shards_of)[partner]
    strong = (owner == chosen) | (owner == (partner + shards_of // 2) % shards_of)
    return jnp.where(strong, factor * drawn, drawn)


def block_levels(key, shape, shards, smallest, largest):
    level, own = 1.0, jax.random.fold_in(key, 6)
    for dim, blocks in shards:
        heights = jnp.exp(jax.random.uniform(jax.random.fold_in(own, dim), (blocks,), jnp.float32, smallest / len(shards), largest / len(shards)))
        level = level * jnp.repeat(heights, shape[dim] // blocks).reshape([-1 if axis == dim else 1 for axis in range(len(shape))])
    return level


def different_ones(stream_key, rows, count, top, lift):
    order = jax.random.permutation(jax.random.fold_in(stream_key, 1), count)
    favour = order
    for power in range(3):
        favour = favour * favour // count
    favour = favour * lift // count
    chance = jax.random.randint(jax.random.fold_in(stream_key, 2), (rows, count), 0, 4096) + favour
    fixed_rows = jax.random.permutation(jax.random.fold_in(stream_key, 3), rows)[jnp.arange(count) % rows]
    chance = jnp.where(jnp.arange(rows)[:, None] == fixed_rows[None, :], 1 << 14, chance)
    priority = chance * count + jnp.arange(count)
    return lax.top_k(priority.astype(jnp.int32), top)[1].astype(jnp.int32)


def bell_draw(key, dims, deviation, limit, cuts=(), kind=jnp.bfloat16):
    factor_of = block_levels(key, dims, cuts, -0.22, 0.18) if cuts else 1.0
    result = jax.random.normal(key, dims, jnp.float32) * deviation * factor_of
    return jnp.minimum(jnp.maximum(result, -limit), limit).astype(kind)


def bell_draw_with(rng, extent, spread, limit, cuts, heavy, kind=jnp.bfloat16):
    values = spread * jax.random.normal(rng, extent, jnp.float32)
    if cuts:
        values = values * block_levels(rng, extent, cuts, -0.22, 0.18)
    return jnp.clip(with_spikes(values, jax.random.fold_in(rng, 3), *heavy), -limit, limit).astype(kind)


def setup_inputs(seed: int = 0) -> dict:
    splits = jax.random.split(jax.random.key(seed), 18)
    return {
        "query_latent": draw_query_latent(jax.random.fold_in(splits[17], 71), 0),
        "query_rope": draw_query_rope(jax.random.fold_in(splits[17], 71), 0),
        "cache_latent": bell_draw(splits[2], (REQ, CTX, DL), 4.0, 16.0, ((1, 256),)),
        "cache_rope": draw_cache_rope(jax.random.fold_in(splits[17], 71), 0),
        "suffix_latent": bell_draw(splits[4], (HYPS, SUF, DL), 4.0, 16.0, ((1, 256),)),
        "suffix_rope": bell_draw(splits[5], (HYPS, DR, SUF), 1.0, 6.0, ((2, 256),)),
        "lengths": draw_lengths(jax.random.fold_in(splits[17], 71), 0),
        "parents": draw_parents(jax.random.fold_in(splits[17], 71), 0),
        "w_uv": bell_draw(splits[8], (DL, H * DV), 0.088, 1.25, ((1, 256),)),
        "w_o": bell_draw(splits[9], (H * DV, D), (H * DV) ** -0.5, 0.046875, ((0, 256),)),
        "hidden": bell_draw(splits[10], (HYPS, D), 1.0, 6.0),
        "norm_gain": jnp.clip(1.0 + 0.18 * jax.random.normal(splits[11], (D,), jnp.float32), 0.1, 1.9),
        "w_gate": bell_draw(splits[12], (EXPERTS * EFF, D), D ** -0.5, 0.0625, ((0, 256),)),
        "w_up": bell_draw(splits[13], (EXPERTS * EFF, D), D ** -0.5, 0.0625, ((0, 256),)),
        "w_down": bell_draw_with(splits[14], (EXPERTS * EFF, D), EFF ** -0.5, 0.5, ((0, 256),), (0, 1, 256, 6.0)),
        "expert_ids": different_ones(splits[15], HYPS, EXPERTS, TOP, 4096),
        "gate_weights": jnp.clip(jax.random.uniform(splits[16], (HYPS, TOP), jnp.float32, 0.1, 0.6), 0.1, 0.6),
    }


MSCALE = 1.0 + 0.1 * math.log(40.0)
NEG = -1e+30

def reference(query_latent, query_rope, cache_latent, cache_rope, suffix_latent, suffix_rope, lengths, parents, w_uv, w_o, hidden, norm_gain, w_gate, w_up, w_down, expert_ids, gate_weights):
    softmax_scale = MSCALE * MSCALE / math.sqrt(DN + DR)
    q_lat = query_latent.astype(jnp.float32)
    q_rope = query_rope.reshape(HYPS, H, DR).astype(jnp.float32)
    request_of = (jnp.arange(HYPS, dtype=jnp.int32) // BEAMS).astype(jnp.int32)
    hyp_length = lengths[request_of]

    def group_step(carry, group):
        run_max, run_sum, run_acc = carry
        pre_start = (group * CTX_DEV).astype(jnp.int32)
        suf_start = (group * SUF_DEV).astype(jnp.int32)
        pre_lat = lax.dynamic_slice_in_dim(cache_latent, pre_start, CTX_DEV, 1)[request_of].astype(jnp.float32)
        pre_rope = lax.dynamic_slice_in_dim(cache_rope, pre_start, CTX_DEV, 2)[request_of].astype(jnp.float32)
        suf_lat = lax.dynamic_slice_in_dim(suffix_latent, suf_start, SUF_DEV, 1)[parents].astype(jnp.float32)
        suf_rope = lax.dynamic_slice_in_dim(suffix_rope, suf_start, SUF_DEV, 2)[parents].astype(jnp.float32)
        keys_lat = jnp.concatenate([pre_lat, suf_lat], axis=1)
        keys_rope = jnp.concatenate([pre_rope, suf_rope], axis=2)
        scores = jnp.einsum('bhl,bsl->bhs', q_lat, keys_lat) + jnp.einsum('bhr,brs->bhs', q_rope, keys_rope)
        scores = scores * softmax_scale
        position = pre_start + jnp.arange(CTX_DEV, dtype=jnp.int32)
        pre_live = position[None, :] < hyp_length[:, None]
        is_live = jnp.concatenate([pre_live, jnp.ones((HYPS, SUF_DEV), dtype=bool)], axis=1)
        scores = jnp.where(is_live[:, None, :], scores, NEG)
        local_max = lax.optimization_barrier(jnp.max(scores, axis=2))
        weights = jnp.exp(scores - local_max[:, :, None]).astype(jnp.bfloat16).astype(jnp.float32)
        weight_sum = lax.optimization_barrier(jnp.sum(weights, axis=2))
        weighted = jnp.einsum('bhs,bsl->bhl', weights, keys_lat)
        new_max = jnp.maximum(run_max, local_max)
        old_factor = jnp.exp(run_max - new_max)
        new_factor = jnp.exp(local_max - new_max)
        run_sum = run_sum * old_factor + weight_sum * new_factor
        run_acc = run_acc * old_factor[:, :, None] + weighted * new_factor[:, :, None]
        return ((new_max, run_sum, run_acc), None)
    start_carry = (jnp.full((HYPS, H), NEG, jnp.float32), jnp.zeros((HYPS, H), jnp.float32), jnp.zeros((HYPS, H, DL), jnp.float32))
    (run_max, run_sum, run_acc), unused = lax.scan(group_step, start_carry, jnp.arange(DEVICES, dtype=jnp.int32))
    attention = (run_acc / run_sum[:, :, None]).astype(jnp.bfloat16)
    value_map = w_uv.astype(jnp.float32).reshape(DL, H, DV)
    values = jnp.einsum('bhl,lhd->bhd', attention.astype(jnp.float32), value_map)
    values = values.astype(jnp.bfloat16).reshape(HYPS, H * DV)
    attended = jnp.dot(values, w_o, preferred_element_type=jnp.float32).astype(jnp.bfloat16)
    residual = hidden.astype(jnp.float32) + attended.astype(jnp.float32)
    mean_square = lax.optimization_barrier(jnp.mean(residual * residual, axis=1, keepdims=True))
    normed = (residual * lax.rsqrt(mean_square + 1e-06) * norm_gain).astype(jnp.bfloat16)

    def expert_step(moe_sum, expert):
        first_row = (expert * EFF).astype(jnp.int32)
        gate_rows = lax.dynamic_slice_in_dim(w_gate, first_row, EFF, 0)
        up_rows = lax.dynamic_slice_in_dim(w_up, first_row, EFF, 0)
        down_rows = lax.dynamic_slice_in_dim(w_down, first_row, EFF, 0)
        routed = lax.optimization_barrier(jnp.sum(gate_weights * (expert_ids == expert).astype(jnp.float32), axis=1))
        gate_out = jnp.dot(normed, gate_rows.T, preferred_element_type=jnp.float32)
        up_out = jnp.dot(normed, up_rows.T, preferred_element_type=jnp.float32)
        activated = (jax.nn.silu(gate_out) * up_out * routed[:, None]).astype(jnp.bfloat16)
        return (moe_sum + jnp.dot(activated, down_rows, preferred_element_type=jnp.float32), None)
    moe_sum, unused = lax.scan(expert_step, jnp.zeros((HYPS, D), jnp.float32), jnp.arange(EXPERTS, dtype=jnp.int32))
    updated = (residual + moe_sum).astype(jnp.bfloat16)
    return (attended, updated)
```

```python
import functools
import math

import jax
import jax.numpy as jnp
from jax import lax
from jax.experimental import pallas as pl
from jax.experimental.pallas import tpu as pltpu
from jax.sharding import PartitionSpec as P

MESH = pl.DeviceIdType.MESH
F32 = jnp.float32
BF16 = jnp.bfloat16

DL = 512
DR = 64
DN = 128
D = 7168
HYPS = 16
HEADS = 128
MSCALE = 1.0 + 0.1 * math.log(40.0)
SCALE = MSCALE * MSCALE / math.sqrt(DN + DR) * math.log2(math.e)
NEG = -1e30
NT = (((1,), (1,)), ((), ()))

N_SEMS = 112
N_LOCAL = 24


def fold(parts):
    top = functools.reduce(jnp.maximum, [p[0] for p in parts])
    total, acc = 0.0, 0.0
    for high, tot, sums in parts:
        factor = jnp.exp2(high - top)
        total = total + tot * factor
        acc = acc + sums * factor
    return top, total, acc


def stat_lanes(columns, rows):
    lane = lax.broadcasted_iota(jnp.int32, (rows, 128), 1)
    out = jnp.zeros((rows, 128), F32)
    for j, column in enumerate(columns):
        out = jnp.where(lane == j, column, out)
    return out


def pack896(part):
    low = jnp.concatenate([part[:, 512:], jnp.zeros((8, 128), part.dtype)], axis=1)
    return jnp.concatenate([part[:, :512], low], axis=0)


def kernel(
    q_hbm, ck_hbm, cr_hbm, sl_hbm, sr_hbm, wuv_hbm, wo_hbm, wg_hbm, wu_hbm, wd_hbm,
    len_ref, par_ref, hid_ref, gain_ref, ids_ref, gw_ref,
    att_ref, upd_ref,
    qv, kv, kr, s0, s1, sr0, sr1, wuv, wo, wg, wu, wd,
    ob, st, xr, xst, ya, yst, yb, ysb, yr, ysr, zt, zsb, zr,
    csb, cr1, c2, c3, c3o, res, nrm, esb, er1, e2f, e2b, er2, e3b, er3,
    ss, rs, ls,
):
    ctx, hx = lax.axis_index("ctx"), lax.axis_index("hx")
    x, z = lax.div(ctx, 8), lax.rem(ctx, 8)
    y, k = lax.div(hx, 2), lax.rem(hx, 2)
    chip = ctx * 4 + y

    def dev(dx=0, dy=0, dz=0, dk=0):
        xx, yy = lax.rem(x + dx, 4), lax.rem(y + dy, 4)
        zz, kk = lax.rem(z + dz, 8), lax.rem(k + dk, 2)
        return (xx * 8 + zz, yy * 2 + kk)

    count = [0, 0]
    sends = []

    def remote(src, dst, where):
        i = count[0]
        count[0] += 1
        copy = pltpu.make_async_remote_copy(
            src_ref=src, dst_ref=dst, send_sem=ss.at[i], recv_sem=rs.at[i],
            device_id=where, device_id_type=MESH,
        )
        copy.start()
        sends.append(copy)
        return copy

    def local(src, dst):
        i = count[1]
        count[1] += 1
        copy = pltpu.make_async_copy(src, dst, ls.at[i])
        copy.start()
        return copy

    kk = 1 - k
    head_rows = pl.ds(pl.multiple_of(hx * 16, 16), 16)
    key_rows = pl.ds(pl.multiple_of(k * 512, 512), 512)
    suf_rows = pl.ds(pl.multiple_of(k * 128, 128), 128)
    uo_rows = pl.ds(pl.multiple_of(k * 64, 64), 64)
    unit_rows = pl.ds(pl.multiple_of(k * 128, 128), 128)
    sv, srv = (s0, s1), (sr0, sr1)

    def kv_pairs(r, core):
        return (
            (ck_hbm.at[2 * core + r], kv.at[r, key_rows]),
            (sl_hbm.at[pl.ds(8 * core + 4 * r, 4)], sv[r].at[:, suf_rows]),
            (cr_hbm.at[2 * core + r], kr.at[r, :, key_rows]),
            (sr_hbm.at[pl.ds(8 * core + 4 * r, 4)], srv[r].at[:, :, suf_rows]),
        )

    w_pairs = (
        (wuv_hbm, wuv.at[k]),
        (wo_hbm, wo.at[uo_rows]),
        (wg_hbm, wg.at[unit_rows]),
        (wu_hbm, wu.at[unit_rows]),
        (wd_hbm, wd.at[unit_rows]),
    )

    HX = [(dy, dk) for dy in (1, 3, 2, 0) for dk in range(2) if dy or dk]
    XY = [(dx, dy) for dx in range(4) for dy in range(4) if dx or dy]

    barrier = pltpu.get_barrier_semaphore()
    peers = [dev(dy=dy, dk=1) for dy in range(4)]
    peers += [dev(dx=dx, dy=dy) for dx, dy in XY]
    peers += [dev(dz=dz) for dz in range(1, 8)]
    for peer in peers:
        pl.semaphore_signal(barrier, inc=1, device_id=peer, device_id_type=MESH)
    own = []
    for r in range(2):
        own.append([local(q_hbm.at[pl.ds(8 * k + 4 * r, 4)], qv.at[pl.ds(4 * r, 4), head_rows])])
        own[r] += [local(src, dst) for src, dst in kv_pairs(r, k)]
    own_w = [local(src, dst) for src, dst in w_pairs]
    pl.semaphore_wait(barrier, len(peers))

    def send_inputs(r):
        got = []
        for dy, dk in HX:
            core = lax.rem(k + dk, 2)
            src = q_hbm.at[pl.ds(8 * core + 4 * r, 4)]
            got.append(remote(src, qv.at[pl.ds(4 * r, 4), head_rows], dev(dy=dy, dk=dk)))
        for src, dst in kv_pairs(r, kk):
            got.append(remote(src, dst, dev(dk=1)))
        return got

    got_in = [send_inputs(0), send_inputs(1)]
    got_w = [remote(src, dst, dev(dk=1)) for src, dst in w_pairs]

    def attend(r):
        for copy in own[r]:
            copy.wait()
        for copy in got_in[r]:
            copy.wait_recv()
        q = qv[4 * r : 4 * r + 4]
        ql = q[..., :DL].reshape(4 * HEADS, DL)
        qr = q[..., DL : DL + DR].reshape(4 * HEADS, DR)
        s = lax.dot_general(ql, kv[r], NT, preferred_element_type=F32)
        s = s + jnp.dot(qr, kr[r], preferred_element_type=F32)
        pos = chip * 1024 + lax.broadcasted_iota(jnp.int32, (1, 1024), 1)
        s = jnp.where(pos < len_ref[2 * k + r], s * SCALE, NEG)
        high = jnp.max(s, axis=1, keepdims=True)
        rows = [slice(i * HEADS, (i + 1) * HEADS) for i in range(4)]
        own_s, tops, parent = [], [], []
        for i in range(4):
            p = lax.rem(par_ref[8 * k + 4 * r + i], 4)
            si = lax.dot_general(q[i, :, :DL], sv[r][p], NT, preferred_element_type=F32)
            si = si + jnp.dot(q[i, :, DL : DL + DR], srv[r][p], preferred_element_type=F32)
            own_s.append(si * SCALE)
            tops.append(jnp.maximum(high[rows[i]], jnp.max(own_s[i], axis=1, keepdims=True)))
            parent.append(p)
        w = jnp.exp2(s - jnp.concatenate(tops, axis=0)).astype(BF16)
        total = jnp.sum(w.astype(F32), axis=1, keepdims=True)
        acc = jnp.dot(w, kv[r], preferred_element_type=F32)
        totals = []
        for i in range(4):
            wi = jnp.exp2(own_s[i] - tops[i]).astype(BF16)
            totals.append(total[rows[i]] + jnp.sum(wi.astype(F32), axis=1, keepdims=True))
            ai = acc[rows[i]] + jnp.dot(wi, sv[r][parent[i]], preferred_element_type=F32)
            ob[4 * r + i] = ai.astype(BF16)
        st[r] = stat_lanes(tops + totals, HEADS)

    def x_send(r):
        got = []
        for dx in (1, 3, 2):
            rows = pl.ds(pl.multiple_of(lax.rem(x + dx, 4) * 32, 32), 32)
            got.append(remote(ob.at[pl.ds(4 * r, 4), rows], xr.at[r, dx - 1], dev(dx=dx)))
            got.append(remote(st.at[r, rows], xst.at[r, dx - 1], dev(dx=dx)))
        return got

    def x_sum(r, got):
        for copy in got:
            copy.wait_recv()
        rows = pl.ds(pl.multiple_of(x * 32, 32), 32)
        stats = [st[r, rows]] + [xst[r, j] for j in range(3)]
        tops, totals = [], []
        for i in range(4):
            sums = [ob[4 * r + i, rows]] + [xr[r, j, i] for j in range(3)]
            parts = [
                (t[:, i : i + 1], t[:, 4 + i : 5 + i], a.astype(F32))
                for t, a in zip(stats, sums)
            ]
            top, total, acc = fold(parts)
            for l in range(4):
                ya[r, i, l] = acc[:, 128 * l : 128 * l + 128]
            tops.append(top)
            totals.append(total)
        yst[r] = stat_lanes(tops + totals, 32)
        for d in range(4):
            pick = pl.ds(d, 8, stride=4)
            for l in range(4):
                block = jnp.concatenate([ya[r, i, l, pick, :] for i in range(4)], axis=0)
                yb[r, d, :, 128 * l : 128 * l + 128] = block.astype(BF16)
            ysb[r, d] = yst[r, pick, :]

    def y_send(r):
        got = []
        for dy in (1, 3, 2):
            to = lax.rem(y + dy, 4)
            got.append(remote(yb.at[r, to], yr.at[r, dy - 1], dev(dy=dy)))
            got.append(remote(ysb.at[r, to], ysr.at[r, dy - 1], dev(dy=dy)))
        return got

    def y_sum(r, got):
        for copy in got:
            copy.wait_recv()
        stats = [ysb[r, y]] + [ysr[r, j] for j in range(3)]
        sums = [yb[r, y].astype(F32)] + [yr[r, j].astype(F32) for j in range(3)]
        for i in range(4):
            parts = [
                (t[:, i : i + 1], t[:, 4 + i : 5 + i], a[8 * i : 8 * i + 8])
                for t, a in zip(stats, sums)
            ]
            top, total, acc = fold(parts)
            at = pl.ds((4 * r + i) * 8, 8)
            for l in range(4):
                zt[l, at] = acc[:, 128 * l : 128 * l + 128]
            zt[4, at] = stat_lanes([top, total], 8)

    attend(0)
    got_x0 = x_send(0)
    attend(1)
    got_x1 = x_send(1)
    x_sum(0, got_x0)
    got_y0 = y_send(0)
    x_sum(1, got_x1)
    got_y1 = y_send(1)
    y_sum(0, got_y0)
    y_sum(1, got_y1)
    for b in range(8):
        for l in range(5):
            zsb[b, :, 128 * l : 128 * l + 128] = zt[l, pl.ds(b, 8, stride=8), :]
    got = []
    for dz in (4, 3, 5, 2, 6, 1, 7):
        got.append(remote(zsb.at[lax.rem(z + dz, 8)], zr.at[dz - 1], dev(dz=dz)))
    for copy in got:
        copy.wait_recv()
    parts = []
    for a in [zsb[z]] + [zr[j] for j in range(7)]:
        parts.append((a[:, DL : DL + 1], a[:, DL + 1 : DL + 2], a[:, :DL]))
    top, total, acc = fold(parts)
    attention = (acc / total).astype(BF16)

    for copy in own_w[:2]:
        copy.wait()
    for copy in got_w[:2]:
        copy.wait_recv()
    v0 = jnp.dot(attention, wuv[0], preferred_element_type=F32).astype(BF16)
    v1 = jnp.dot(attention, wuv[1], preferred_element_type=F32).astype(BF16)
    for b in range(8):
        cols = slice(896 * b, 896 * b + 896)
        term = jnp.dot(v0, wo[:64, cols], preferred_element_type=F32)
        term = term + jnp.dot(v1, wo[64:, cols], preferred_element_type=F32)
        csb[b] = pack896(term).astype(BF16)
    got = []
    for dz in (4, 3, 5, 2, 6, 1, 7):
        got.append(remote(csb.at[lax.rem(z + dz, 8)], cr1.at[dz - 1], dev(dz=dz)))
    for copy in got:
        copy.wait_recv()
    part = csb[z].astype(F32)
    for j in range(7):
        part = part + cr1[j].astype(F32)
    me = x * 4 + y
    c2[me] = part.astype(BF16)
    got = []
    for dx, dy in sorted(XY, key=lambda d: -(min(d[0], 4 - d[0]) + min(d[1], 4 - d[1]))):
        got.append(remote(c2.at[me], c2.at[me], dev(dx=dx, dy=dy)))
    for copy in got:
        copy.wait_recv()
    part = c2[0].astype(F32)
    for j in range(1, 16):
        part = part + c2[j].astype(F32)
    c3[z] = part.astype(BF16)
    got = []
    for dz in (4, 3, 5, 2, 6, 1, 7):
        got.append(remote(c3.at[z], c3.at[z], dev(dz=dz)))
    for copy in got:
        copy.wait_recv()
    got_att = remote(c3, c3o, dev(dk=1))

    square = jnp.zeros((8, 1), F32)
    for b in range(8):
        block = c3[b].astype(F32)
        for half, width in ((0, 512), (1, 384)):
            cols = slice(896 * b + 512 * half, 896 * b + 512 * half + width)
            hid = hid_ref[:, cols].astype(F32)
            hid = jnp.where(k == 0, hid[:8], hid[8:])
            value = hid + block[8 * half : 8 * half + 8, :width]
            res[:, cols] = value
            square = square + jnp.sum(value * value, axis=1, keepdims=True)
    scale = lax.rsqrt(square / D + 1e-6)
    nrm[...] = (res[...] * scale * gain_ref[...]).astype(BF16)

    expert = lax.div(ctx, 2)
    route = jnp.sum(gw_ref[...] * (ids_ref[...] == expert).astype(F32), axis=1, keepdims=True)
    route = jnp.where(k == 0, route[:8], route[8:])
    for copy in own_w[2:]:
        copy.wait()
    for copy in got_w[2:]:
        copy.wait_recv()
    gate = lax.dot_general(nrm[...], wg[...], NT, preferred_element_type=F32)
    up = lax.dot_general(nrm[...], wu[...], NT, preferred_element_type=F32)
    act = (gate / (1.0 + jnp.exp(-gate)) * up * route).astype(BF16)
    for b in range(4):
        cols = slice(1792 * b, 1792 * b + 1792)
        term = jnp.dot(act, wd[:, cols], preferred_element_type=F32)
        esb[b] = jnp.concatenate([term[:, :896], term[:, 896:]], axis=0).astype(BF16)
    got = []
    for dx in (2, 1, 3):
        got.append(remote(esb.at[lax.rem(x + dx, 4)], er1.at[dx - 1], dev(dx=dx)))
    for copy in got:
        copy.wait_recv()
    part = esb[x].astype(F32)
    for j in range(3):
        part = part + er1[j].astype(F32)
    part = jnp.concatenate([part[:8], part[8:]], axis=1)
    lane = lax.broadcasted_iota(jnp.int32, (8, 1792), 1)
    mine = (lane >= z * 224) & (lane < z * 224 + 224) & (y == 0)
    rest = res[:, pl.ds(pl.multiple_of(x * 1792, 128), 1792)]
    part = part + jnp.where(mine, rest, 0.0)
    for b in range(8):
        piece = part[:, 224 * b : 224 * b + 224]
        piece = jnp.concatenate([piece, jnp.zeros((8, 32), F32)], axis=1)
        e2f[b] = piece
        e2b[b] = jnp.concatenate([piece[:, :128], piece[:, 128:]], axis=0).astype(BF16)
    got = []
    for dz in (4, 3, 5, 2, 6, 1, 7):
        got.append(remote(e2b.at[lax.rem(z + dz, 8)], er2.at[dz - 1], dev(dz=dz)))
    for copy in got:
        copy.wait_recv()
    part = er2[0].astype(F32)
    for j in range(1, 7):
        part = part + er2[j].astype(F32)
    part = jnp.concatenate([part[:8], part[8:]], axis=1) + e2f[z]
    for b in range(8):
        piece = part[:, 28 * b : 28 * b + 28]
        e3b[b] = jnp.concatenate([piece, jnp.zeros((8, 100), F32)], axis=1)
    got = []
    for dy, dk in HX:
        to = lax.rem(y + dy, 4) * 2 + lax.rem(k + dk, 2)
        got.append(remote(e3b.at[to], er3.at[2 * dy + dk], dev(dy=dy, dk=dk)))
    for copy in got:
        copy.wait_recv()
    same = e3b[hx] + er3[2] + er3[4] + er3[6]
    other = er3[1] + er3[3] + er3[5] + er3[7]
    both = jnp.concatenate(
        [jnp.where(k == 0, same, other), jnp.where(k == 0, other, same)], axis=0
    )
    upd_ref[...] = both[:, :28].astype(BF16)

    got_att.wait_recv()
    for b in range(8):
        a, o = c3[b].astype(F32), c3o[b].astype(F32)
        first, second = jnp.where(k == 0, a, o), jnp.where(k == 0, o, a)
        for half, width in ((0, 512), (1, 384)):
            cols = slice(896 * b + 512 * half, 896 * b + 512 * half + width)
            rows = slice(8 * half, 8 * half + 8)
            pair = jnp.concatenate([first[rows, :width], second[rows, :width]], axis=0)
            att_ref[:, cols] = pair.astype(BF16)
    for copy in sends:
        copy.wait_send()


def local(
    query_latent, query_rope, cache_latent, cache_rope, suffix_latent, suffix_rope, lengths,
    parents, w_uv, w_o, hidden, norm_gain, w_gate, w_up, w_down, expert_ids, gate_weights,
):
    q = jnp.concatenate([query_latent, query_rope.reshape(HYPS, 16, DR)], axis=2)
    hbm = pl.BlockSpec(memory_space=pl.ANY)
    vmem = pl.BlockSpec(memory_space=pltpu.VMEM)
    smem = pl.BlockSpec(memory_space=pltpu.SMEM)
    scratch = [
        ((8, 128, DL + DR), BF16),
        ((2, 1024, DL), BF16),
        ((2, DR, 1024), BF16),
        ((4, 256, DL), BF16),
        ((4, 256, DL), BF16),
        ((4, DR, 256), BF16),
        ((4, DR, 256), BF16),
        ((2, DL, 64), BF16),
        ((128, D), BF16),
        ((256, D), BF16),
        ((256, D), BF16),
        ((256, D), BF16),
        ((8, 128, DL), BF16),
        ((2, 128, 128), F32),
        ((2, 3, 4, 32, DL), BF16),
        ((2, 3, 32, 128), F32),
        ((2, 4, 4, 32, 128), F32),
        ((2, 32, 128), F32),
        ((2, 4, 32, DL), BF16),
        ((2, 4, 8, 128), F32),
        ((2, 3, 32, DL), BF16),
        ((2, 3, 8, 128), F32),
        ((5, 64, 128), F32),
        ((8, 8, 640), F32),
        ((7, 8, 640), F32),
        ((8, 16, 512), BF16),
        ((7, 16, 512), BF16),
        ((16, 16, 512), BF16),
        ((8, 16, 512), BF16),
        ((8, 16, 512), BF16),
        ((8, D), F32),
        ((8, D), BF16),
        ((4, 16, 896), BF16),
        ((3, 16, 896), BF16),
        ((8, 8, 256), F32),
        ((8, 16, 128), BF16),
        ((7, 16, 128), BF16),
        ((8, 8, 128), F32),
        ((8, 8, 128), F32),
    ]
    return pl.pallas_call(
        kernel,
        name="decode_step",
        out_shape=(
            jax.ShapeDtypeStruct((HYPS, D), BF16),
            jax.ShapeDtypeStruct((HYPS, 28), BF16),
        ),
        in_specs=[hbm] * 10 + [smem] * 2 + [vmem] * 4,
        out_specs=(vmem, vmem),
        scratch_shapes=[pltpu.VMEM(shape, dtype) for shape, dtype in scratch]
        + [
            pltpu.SemaphoreType.DMA((N_SEMS,)),
            pltpu.SemaphoreType.DMA((N_SEMS,)),
            pltpu.SemaphoreType.DMA((N_LOCAL,)),
        ],
        compiler_params=pltpu.CompilerParams(
            collective_id=0, has_side_effects=True, vmem_limit_bytes=48 << 20
        ),
    )(
        q, cache_latent, cache_rope, suffix_latent, suffix_rope, w_uv, w_o, w_gate, w_up, w_down,
        lengths, parents, hidden, norm_gain.reshape(1, D), expert_ids, gate_weights,
    )


def solution(mesh):
    both = ("ctx", "hx")
    in_specs = (
        P(None, "hx", None),
        P(None, "hx"),
        P(None, both, None),
        P(None, None, both),
        P(None, both, None),
        P(None, None, both),
        P(),
        P(),
        P(None, both),
        P(both, None),
        P(),
        P(),
        P(both, None),
        P(both, None),
        P(both, None),
        P(),
        P(),
    )
    out_specs = (P(), P(None, both))
    return jax.shard_map(local, mesh=mesh, in_specs=in_specs, out_specs=out_specs, check_vma=False)
```

```python
import functools
import math

import jax
import jax.numpy as jnp
from jax import lax
from jax.experimental import pallas as pl
from jax.experimental.pallas import tpu as pltpu
from jax.sharding import PartitionSpec as P

MESH = pl.DeviceIdType.MESH
F32 = jnp.float32
BF16 = jnp.bfloat16

DL = 512
DR = 64
DN = 128
D = 7168
HYPS = 16
HEADS = 128
MSCALE = 1.0 + 0.1 * math.log(40.0)
SCALE = MSCALE * MSCALE / math.sqrt(DN + DR) * math.log2(math.e)
NEG = -1e30
NT = (((1,), (1,)), ((), ()))

N_SEMS = 168
N_LOCAL = 24


def fold(parts):
    top = functools.reduce(jnp.maximum, [p[0] for p in parts])
    total, acc = 0.0, 0.0
    for high, tot, sums in parts:
        factor = jnp.exp2(high - top)
        total = total + tot * factor
        acc = acc + sums * factor
    return top, total, acc


def stat_lanes(columns, rows):
    lane = lax.broadcasted_iota(jnp.int32, (rows, 128), 1)
    out = jnp.zeros((rows, 128), F32)
    for j, column in enumerate(columns):
        out = jnp.where(lane == j, column, out)
    return out


def window(tiles, start, dest):
    at, off = divmod(start, 128)
    shift = (dest - off) % 128
    out = pltpu.roll(tiles[at], shift, 1) if shift else tiles[at]
    if off + 56 > 128:
        lane = lax.broadcasted_iota(jnp.int32, (8, 128), 1)
        after = pltpu.roll(tiles[at + 1], shift, 1) if shift else tiles[at + 1]
        out = jnp.where(lane < dest + 128 - off, out, after)
    return out


def pack896(part):
    low = jnp.concatenate([part[:, 512:], jnp.zeros((8, 128), part.dtype)], axis=1)
    return jnp.concatenate([part[:, :512], low], axis=0)


def kernel(
    ql_hbm, qr_hbm, ck_hbm, cr_hbm, sl_hbm, sr_hbm, wuv_hbm, wo_hbm, wg_hbm, wu_hbm, wd_hbm,
    len_hbm, par_hbm, hid_hbm, gain_hbm, ids_hbm, gw_hbm,
    att_ref, upd_ref,
    hid_ref, gain_ref, ids_ref, gw_ref, rope, ropes, qc, qv0, qv1, kv, kr, s0, s1, sr0, sr1,
    wuv, wo, wg, wu, wd, tmp, st, ob, osb, br, bsr, zt, zsb, zr,
    csb, cr1, c2, c3, c3o, res, nrm, e1f, esb, er1, e2b, er2,
    len_ref, par_ref, ss, rs, ls,
):
    ctx, hx = lax.axis_index("ctx"), lax.axis_index("hx")
    x, z = lax.div(ctx, 8), lax.rem(ctx, 8)
    y, k = lax.div(hx, 2), lax.rem(hx, 2)
    chip = ctx * 4 + y

    def dev(dx=0, dy=0, dz=0, dk=0):
        xx, yy = lax.rem(x + dx, 4), lax.rem(y + dy, 4)
        zz, kk = lax.rem(z + dz, 8), lax.rem(k + dk, 2)
        return (xx * 8 + zz, yy * 2 + kk)

    count = [0, 0]
    sends = []

    def remote(src, dst, where):
        i = count[0]
        count[0] += 1
        copy = pltpu.make_async_remote_copy(
            src_ref=src, dst_ref=dst, send_sem=ss.at[i], recv_sem=rs.at[i],
            device_id=where, device_id_type=MESH,
        )
        copy.start()
        sends.append(copy)
        return copy

    def local(src, dst):
        i = count[1]
        count[1] += 1
        copy = pltpu.make_async_copy(src, dst, ls.at[i])
        copy.start()
        return copy

    kk = 1 - k
    head_rows = pl.ds(pl.multiple_of(hx * 16, 16), 16)
    key_rows = pl.ds(pl.multiple_of(k * 512, 512), 512)
    suf_rows = pl.ds(pl.multiple_of(k * 128, 128), 128)
    uo_rows = pl.ds(pl.multiple_of(k * 64, 64), 64)
    unit_rows = pl.ds(pl.multiple_of(k * 128, 128), 128)
    sv, srv = (s0, s1), (sr0, sr1)

    def kv_pairs(r, core):
        rows = slice(DR * r, DR * r + DR)
        return (
            (ck_hbm.at[2 * core + r], kv.at[r, key_rows]),
            (sl_hbm.at[pl.ds(8 * core + 4 * r, 4)], sv[r].at[:, suf_rows]),
            (cr_hbm.at[2 * core + r], kr.at[r, rows, key_rows]),
            (sr_hbm.at[pl.ds(8 * core + 4 * r, 4)], srv[r].at[:, rows, suf_rows]),
        )

    w_pairs = (
        (wuv_hbm, wuv.at[k]),
        (wo_hbm, wo.at[uo_rows]),
        (wg_hbm, wg.at[unit_rows]),
        (wu_hbm, wu.at[unit_rows]),
        (wd_hbm, wd.at[unit_rows]),
    )

    HX = [(dy, dk) for dy in (1, 3, 2, 0) for dk in range(2) if dy or dk]
    XY = [(dx, dy) for dx in range(4) for dy in range(4) if dx or dy]
    XY.sort(key=lambda d: -min(d[0], 4 - d[0]) - min(d[1], 4 - d[1]))
    ZK = [(dz, dk) for dz in (4, 3, 5, 2, 6, 1, 7, 0) for dk in range(2) if dz or dk]

    barrier = pltpu.get_barrier_semaphore()
    peers = [dev(dz=dz, dk=dk) for dz, dk in ZK]
    peers += [dev(dx=dx, dy=dy) for dx, dy in XY]
    peers += [dev(dy=dy, dk=1) for dy in range(1, 4)]
    for peer in peers:
        pl.semaphore_signal(barrier, inc=1, device_id=peer, device_id_type=MESH)
    own_q = [local(qr_hbm, rope)]
    own_q += [local(ql_hbm.at[pl.ds(8 * c, 4)], qc.at[c, :, :, :DL]) for c in range(2)]
    own = [[local(src, dst) for src, dst in kv_pairs(r, k)] for r in range(2)]
    own[0] += [local(len_hbm, len_ref), local(par_hbm, par_ref)]
    own[1].append(local(ql_hbm.at[pl.ds(8 * k + 4, 4)], qv1.at[:, head_rows]))
    own_w = [local(src, dst) for src, dst in w_pairs]
    small = [(hid_hbm, hid_ref), (gain_hbm, gain_ref), (ids_hbm, ids_ref), (gw_hbm, gw_ref)]
    own_small = [local(src, dst) for src, dst in small]
    kr[0, DR:] = jnp.zeros((DR, 1024), BF16)
    kr[1, :DR] = jnp.zeros((DR, 1024), BF16)
    sr0[:, DR:] = jnp.zeros((4, DR, 256), BF16)
    sr1[:, :DR] = jnp.zeros((4, DR, 256), BF16)
    own_q[0].wait()
    low = lax.broadcasted_iota(jnp.int32, (16, 128), 1) < DR
    for t in range(8):
        pair = rope[:, 128 * t : 128 * t + 128].astype(F32)
        swap = pltpu.roll(pair, DR, 1)
        ropes[pl.ds(2 * t, 16, stride=16), :] = jnp.where(low, pair, pltpu.roll(swap, 12, 0))
        ropes[pl.ds(2 * t + 1, 16, stride=16), :] = jnp.where(low, swap, pltpu.roll(pair, 12, 0))
    for c in range(2):
        for i in range(4):
            row = 16 * (8 * c + i)
            qc[c, i, :, DL:] = ropes[row : row + 16, :].astype(BF16)
    own_q[1].wait()
    own_q[2].wait()
    own[0].append(local(qc.at[k], qv0.at[:, head_rows]))
    pl.semaphore_wait(barrier, len(peers))

    beam = lax.rem(x + 2 * z, 4)
    got_q = {}
    for dy, dk in HX:
        core = lax.rem(k + dk, 2)
        if dy:
            src, dst = qc.at[core, beam], qv0.at[beam, head_rows]
        else:
            src, dst = qc.at[core], qv0.at[:, head_rows]
        got_q[dy, dk] = remote(src, dst, dev(dy=dy, dk=dk))
    got_in = [[got_q[0, 1]], []]
    for src, dst in kv_pairs(0, kk):
        got_in[0].append(remote(src, dst, dev(dk=1)))
    for dy in (1, 3, 2):
        for copy in (got_q[dy, 0], got_q[dy, 1]):
            copy.wait_recv()
        rows = pl.ds(pl.multiple_of(lax.rem(y + 4 - dy, 4) * 32, 32), 32)
        block = qv0.at[beam, rows]
        for where in (dev(dx=1), dev(dx=3), dev(dz=1)):
            got_in[0].append(remote(block, block, where))

    for dy, dk in HX:
        core = lax.rem(k + dk, 2)
        src = ql_hbm.at[pl.ds(8 * core + 4, 4)]
        got_in[1].append(remote(src, qv1.at[:, head_rows], dev(dy=dy, dk=dk)))
    for src, dst in kv_pairs(1, kk):
        got_in[1].append(remote(src, dst, dev(dk=1)))
    def attend(r):
        for copy in own[r]:
            copy.wait()
        for copy in got_in[r]:
            copy.wait_recv()
        q = qv0[..., :DL] if r == 0 else qv1[...]
        qr = qv0[..., DL:]
        ql = q.reshape(4 * HEADS, DL)
        s = lax.dot_general(ql, kv[r], NT, preferred_element_type=F32)
        s = s + jnp.dot(
            qr.reshape(4 * HEADS, 128), kr[r], preferred_element_type=F32
        )
        pos = chip * 1024 + lax.broadcasted_iota(jnp.int32, (1, 1024), 1)
        s = jnp.where(pos < len_ref[2 * k + r], s * SCALE, NEG)
        high = jnp.max(s, axis=1, keepdims=True)
        rows = [slice(i * HEADS, (i + 1) * HEADS) for i in range(4)]
        own_s, tops, parent = [], [], []
        for i in range(4):
            p = lax.rem(par_ref[8 * k + 4 * r + i], 4)
            si = lax.dot_general(q[i], sv[r][p], NT, preferred_element_type=F32)
            si = si + jnp.dot(qr[i], srv[r][p], preferred_element_type=F32)
            own_s.append(si * SCALE)
            tops.append(jnp.maximum(high[rows[i]], jnp.max(own_s[i], axis=1, keepdims=True)))
            parent.append(p)
        w = jnp.exp2(s - jnp.concatenate(tops, axis=0)).astype(BF16)
        total = jnp.sum(w.astype(F32), axis=1, keepdims=True)
        acc = jnp.dot(w, kv[r], preferred_element_type=F32)
        totals = []
        for i in range(4):
            wi = jnp.exp2(own_s[i] - tops[i]).astype(BF16)
            totals.append(total[rows[i]] + jnp.sum(wi.astype(F32), axis=1, keepdims=True))
            ai = acc[rows[i]] + jnp.dot(wi, sv[r][parent[i]], preferred_element_type=F32)
            for l in range(4):
                tmp[i, l] = ai[:, 128 * l : 128 * l + 128]
        st[...] = stat_lanes(tops + totals, HEADS)
        for to in range(16):
            pick = pl.ds(32 * (to // 4) + to % 4, 8, stride=4)
            for l in range(4):
                block = jnp.concatenate([tmp[i, l, pick, :] for i in range(4)], axis=0)
                ob[r, to, :, 128 * l : 128 * l + 128] = block.astype(BF16)
            osb[r, to] = st[pick, :]

    me = x * 4 + y

    def join_send(r):
        got = []
        for j, (dx, dy) in enumerate(XY):
            to = lax.rem(x + dx, 4) * 4 + lax.rem(y + dy, 4)
            got.append(remote(osb.at[r, to], bsr.at[r, j], dev(dx=dx, dy=dy)))
            got.append(remote(ob.at[r, to], br.at[r, j], dev(dx=dx, dy=dy)))
        return got

    def join(r, got):
        for copy in got:
            copy.wait_recv()
        stats = [osb[r, me]] + [bsr[r, j] for j in range(15)]
        top = functools.reduce(jnp.maximum, stats)
        factors = [jnp.exp2(stat - top) for stat in stats]
        total = sum(pltpu.roll(f, 4, 1) * stat for f, stat in zip(factors, stats))
        for i in range(4):
            acc = jnp.zeros((8, DL), F32)
            for j in range(16):
                block = ob[r, me] if j == 0 else br[r, j - 1]
                rows = block.astype(F32)[8 * i : 8 * i + 8]
                acc = acc + rows * factors[j][:, i : i + 1]
            at = pl.ds((4 * r + i) * 8, 8)
            for l in range(4):
                zt[l, at] = acc[:, 128 * l : 128 * l + 128]
            zt[4, at] = stat_lanes([top[:, i : i + 1], total[:, 4 + i : 5 + i]], 8)

    attend(0)
    got_b0 = join_send(0)
    got_w = [remote(src, dst, dev(dk=1)) for src, dst in w_pairs]
    attend(1)
    got_b1 = join_send(1)
    join(0, got_b0)
    join(1, got_b1)
    for b in range(8):
        for l in range(5):
            zsb[b, :, 128 * l : 128 * l + 128] = zt[l, pl.ds(b, 8, stride=8), :]
    got = []
    for dz in (4, 3, 5, 2, 6, 1, 7):
        got.append(remote(zsb.at[lax.rem(z + dz, 8)], zr.at[dz - 1], dev(dz=dz)))
    for copy in got:
        copy.wait_recv()
    parts = []
    for a in [zsb[z]] + [zr[j] for j in range(7)]:
        parts.append((a[:, DL : DL + 1], a[:, DL + 1 : DL + 2], a[:, :DL]))
    top, total, acc = fold(parts)
    attention = (acc / total).astype(BF16)

    for copy in own_w[:2]:
        copy.wait()
    for copy in got_w[:2]:
        copy.wait_recv()
    v0 = lax.dot_general(attention, wuv[0], NT, preferred_element_type=F32).astype(BF16)
    v1 = lax.dot_general(attention, wuv[1], NT, preferred_element_type=F32).astype(BF16)
    for b in range(8):
        cols = slice(896 * b, 896 * b + 896)
        term = jnp.dot(v0, wo[:64, cols], preferred_element_type=F32)
        term = term + jnp.dot(v1, wo[64:, cols], preferred_element_type=F32)
        csb[b] = pack896(term).astype(BF16)
    got = []
    for dz in (4, 3, 5, 2, 6, 1, 7):
        got.append(remote(csb.at[lax.rem(z + dz, 8)], cr1.at[dz - 1], dev(dz=dz)))
    for copy in got:
        copy.wait_recv()
    part = csb[z].astype(F32)
    for j in range(7):
        part = part + cr1[j].astype(F32)
    c2[me] = part.astype(BF16)
    got = []
    for dx, dy in XY:
        got.append(remote(c2.at[me], c2.at[me], dev(dx=dx, dy=dy)))
    for copy in got:
        copy.wait_recv()
    part = c2[0].astype(F32)
    for j in range(1, 16):
        part = part + c2[j].astype(F32)
    c3[z] = part.astype(BF16)
    got = []
    for dz in (4, 3, 5, 2, 6, 1, 7):
        got.append(remote(c3.at[z], c3.at[z], dev(dz=dz)))
    for copy in got:
        copy.wait_recv()
    got_att = remote(c3, c3o, dev(dk=1))

    for copy in own_small:
        copy.wait()
    square = jnp.zeros((8, 1), F32)
    for b in range(8):
        block = c3[b].astype(F32)
        for half, width in ((0, 512), (1, 384)):
            cols = slice(896 * b + 512 * half, 896 * b + 512 * half + width)
            hid = hid_ref[:, cols].astype(F32)
            hid = jnp.where(k == 0, hid[:8], hid[8:])
            value = hid + block[8 * half : 8 * half + 8, :width]
            res[:, cols] = value
            square = square + jnp.sum(value * value, axis=1, keepdims=True)
    scale = lax.rsqrt(square / D + 1e-6)
    nrm[...] = (res[...] * scale * gain_ref[...]).astype(BF16)

    expert = lax.div(ctx, 2)
    route = jnp.sum(gw_ref[...] * (ids_ref[...] == expert).astype(F32), axis=0, keepdims=True)
    row = lax.broadcasted_iota(jnp.int32, (8, HYPS), 0)
    col = lax.broadcasted_iota(jnp.int32, (8, HYPS), 1)
    route = jnp.sum(jnp.where(col == row + 8 * k, route, 0.0), axis=1, keepdims=True)
    for copy in own_w[2:]:
        copy.wait()
    for copy in got_w[2:]:
        copy.wait_recv()
    gate = lax.dot_general(nrm[...], wg[...], NT, preferred_element_type=F32)
    up = lax.dot_general(nrm[...], wu[...], NT, preferred_element_type=F32)
    act = (gate / (1.0 + jnp.exp(-gate)) * up * route).astype(BF16)
    start = x * 1792 + z * 224 + y * 56
    lane = lax.broadcasted_iota(jnp.int32, (8, 128), 1)
    for b in range(4):
        tiles = []
        for t in range(14):
            cols = slice(1792 * b + 128 * t, 1792 * b + 128 * t + 128)
            if t % 7 == 0:
                wide = slice(cols.start, cols.start + 896)
                term = jnp.dot(act, wd[:, wide], preferred_element_type=F32)
            col = lane + cols.start
            mine = (col >= start) & (col < start + 56)
            piece = term[:, 128 * (t % 7) : 128 * (t % 7) + 128]
            tiles.append(piece + jnp.where(mine, res[:, cols], 0.0))
        for c in range(4):
            halves = [
                jnp.where(
                    lane < 64,
                    window(tiles, 448 * u + 56 * c, 0),
                    window(tiles, 448 * u + 224 + 56 * c, 64),
                )
                for u in range(4)
            ]
            whole = jnp.concatenate(halves, axis=1)
            e1f[4 * b + c] = whole
            esb[4 * b + c] = jnp.concatenate([whole[:, :256], whole[:, 256:]], axis=0).astype(BF16)
    got = []
    for j, (dx, dy) in enumerate(XY):
        to = lax.rem(x + dx, 4) * 4 + lax.rem(y + dy, 4)
        got.append(remote(esb.at[to], er1.at[j], dev(dx=dx, dy=dy)))
    for copy in got:
        copy.wait_recv()
    part = er1[0].astype(F32)
    for j in range(1, 15):
        part = part + er1[j].astype(F32)
    part = jnp.concatenate([part[:8], part[8:]], axis=1) + e1f[me]
    for b in range(8):
        tile = part[:, 128 * (b // 2) : 128 * (b // 2) + 128]
        for c in range(2):
            off = 64 * (b % 2) + 28 * c
            e2b[2 * b + c] = pltpu.roll(tile, 128 - off, 1) if off else tile
    got = []
    for j, (dz, dk) in enumerate(ZK):
        to = lax.rem(z + dz, 8) * 2 + lax.rem(k + dk, 2)
        got.append(remote(e2b.at[to], er2.at[j], dev(dz=dz, dk=dk)))
    for copy in got:
        copy.wait_recv()
    same, other = e2b[2 * z + k], jnp.zeros((8, 128), F32)
    for j, (dz, dk) in enumerate(ZK):
        if dk:
            other = other + er2[j]
        else:
            same = same + er2[j]
    both = jnp.concatenate(
        [jnp.where(k == 0, same, other), jnp.where(k == 0, other, same)], axis=0
    )
    upd_ref[...] = both[:, :28].astype(BF16)

    got_att.wait_recv()
    for b in range(8):
        a, o = c3[b].astype(F32), c3o[b].astype(F32)
        first, second = jnp.where(k == 0, a, o), jnp.where(k == 0, o, a)
        for half, width in ((0, 512), (1, 384)):
            cols = slice(896 * b + 512 * half, 896 * b + 512 * half + width)
            rows = slice(8 * half, 8 * half + 8)
            pair = jnp.concatenate([first[rows, :width], second[rows, :width]], axis=0)
            att_ref[:, cols] = pair.astype(BF16)
    for copy in sends:
        copy.wait_send()


def local(
    query_latent, query_rope, cache_latent, cache_rope, suffix_latent, suffix_rope, lengths,
    parents, w_uv, w_o, hidden, norm_gain, w_gate, w_up, w_down, expert_ids, gate_weights,
):
    hbm = pl.BlockSpec(memory_space=pltpu.HBM)
    vmem = pl.BlockSpec(memory_space=pltpu.VMEM)
    scratch = [
        ((HYPS, D), BF16),
        ((1, D), F32),
        ((8, HYPS), jnp.int32),
        ((8, HYPS), F32),
        ((HYPS, 16 * DR), BF16),
        ((256, 128), F32),
        ((2, 4, 16, DL + 128), BF16),
        ((4, 128, DL + 128), BF16),
        ((4, 128, DL), BF16),
        ((2, 1024, DL), BF16),
        ((2, 2 * DR, 1024), BF16),
        ((4, 256, DL), BF16),
        ((4, 256, DL), BF16),
        ((4, 2 * DR, 256), BF16),
        ((4, 2 * DR, 256), BF16),
        ((2, 64, DL), BF16),
        ((128, D), BF16),
        ((256, D), BF16),
        ((256, D), BF16),
        ((256, D), BF16),
        ((4, 4, HEADS, 128), F32),
        ((HEADS, 128), F32),
        ((2, 16, 32, DL), BF16),
        ((2, 16, 8, 128), F32),
        ((2, 15, 32, DL), BF16),
        ((2, 15, 8, 128), F32),
        ((5, 64, 128), F32),
        ((8, 8, 640), F32),
        ((7, 8, 640), F32),
        ((8, 16, 512), BF16),
        ((7, 16, 512), BF16),
        ((16, 16, 512), BF16),
        ((8, 16, 512), BF16),
        ((8, 16, 512), BF16),
        ((8, D), F32),
        ((8, D), BF16),
        ((16, 8, 512), F32),
        ((16, 16, 256), BF16),
        ((15, 16, 256), BF16),
        ((16, 8, 128), F32),
        ((15, 8, 128), F32),
    ]
    return pl.pallas_call(
        kernel,
        name="decode_step",
        out_shape=(
            jax.ShapeDtypeStruct((HYPS, D), BF16),
            jax.ShapeDtypeStruct((HYPS, 28), BF16),
        ),
        in_specs=[hbm] * 17,
        out_specs=(vmem, vmem),
        scratch_shapes=[pltpu.VMEM(shape, dtype) for shape, dtype in scratch]
        + [
            pltpu.SMEM((4,), jnp.int32),
            pltpu.SMEM((16,), jnp.int32),
            pltpu.SemaphoreType.DMA((N_SEMS,)),
            pltpu.SemaphoreType.DMA((N_SEMS,)),
            pltpu.SemaphoreType.DMA((N_LOCAL,)),
        ],
        compiler_params=pltpu.CompilerParams(
            collective_id=0, has_side_effects=True, vmem_limit_bytes=48 << 20
        ),
    )(
        *(
            pltpu.with_memory_space_constraint(value, pltpu.HBM)
            for value in (
                query_latent, query_rope, cache_latent, cache_rope, suffix_latent, suffix_rope,
                w_uv.T, w_o, w_gate, w_up, w_down, lengths, parents, hidden,
                norm_gain.reshape(1, D), expert_ids.T, gate_weights.T,
            )
        )
    )


def solution(mesh):
    both = ("ctx", "hx")
    in_specs = (
        P(None, "hx", None),
        P(None, "hx"),
        P(None, both, None),
        P(None, None, both),
        P(None, both, None),
        P(None, None, both),
        P(),
        P(),
        P(None, both),
        P(both, None),
        P(),
        P(),
        P(both, None),
        P(both, None),
        P(both, None),
        P(),
        P(),
    )
    out_specs = (P(), P(None, both))
    return jax.shard_map(local, mesh=mesh, in_specs=in_specs, out_specs=out_specs, check_vma=False)
```

```python
import functools
import math

import jax
import jax.numpy as jnp
from jax import lax
from jax.experimental import pallas as pl
from jax.experimental.pallas import tpu as pltpu
from jax.sharding import PartitionSpec as P

MESH = pl.DeviceIdType.MESH
F32 = jnp.float32
BF16 = jnp.bfloat16

DL = 512
DR = 64
DN = 128
D = 7168
HYPS = 16
HEADS = 128
MSCALE = 1.0 + 0.1 * math.log(40.0)
SCALE = MSCALE * MSCALE / math.sqrt(DN + DR) * math.log2(math.e)
NEG = -1e30
NT = (((1,), (1,)), ((), ()))

N_SEMS = 168
N_LOCAL = 24


def fold(parts):
    top = functools.reduce(jnp.maximum, [p[0] for p in parts])
    total, acc = 0.0, 0.0
    for high, tot, sums in parts:
        factor = jnp.exp2(high - top)
        total = total + tot * factor
        acc = acc + sums * factor
    return top, total, acc


def stat_lanes(columns, rows):
    lane = lax.broadcasted_iota(jnp.int32, (rows, 128), 1)
    out = jnp.zeros((rows, 128), F32)
    for j, column in enumerate(columns):
        out = jnp.where(lane == j, column, out)
    return out


def window(tiles, start, dest):
    at, off = divmod(start, 128)
    shift = (dest - off) % 128
    out = pltpu.roll(tiles[at], shift, 1) if shift else tiles[at]
    if off + 56 > 128:
        lane = lax.broadcasted_iota(jnp.int32, (8, 128), 1)
        after = pltpu.roll(tiles[at + 1], shift, 1) if shift else tiles[at + 1]
        out = jnp.where(lane < dest + 128 - off, out, after)
    return out


def pack896(part):
    low = jnp.concatenate([part[:, 512:], jnp.zeros((8, 128), part.dtype)], axis=1)
    return jnp.concatenate([part[:, :512], low], axis=0)


def kernel(
    ql_hbm, qr_hbm, ck_hbm, cr_hbm, sl_hbm, sr_hbm, wuv_hbm, wo_hbm, wg_hbm, wu_hbm, wd_hbm,
    len_hbm, par_hbm, hid_hbm, gain_hbm, ids_hbm, gw_hbm,
    att_ref, upd_ref,
    hid_ref, gain_ref, ids_ref, gw_ref, rope, ropes, qc, qv0, qv1, kv, kr, s0, s1, sr0, sr1,
    wuv, wo, wg, wu, wd, tmp, st, ob, osb, br, bsr, zt, zsb, zr,
    csb, cr1, c2, c3, c3o, res, nrm, e1f, esb, er1, e2b, er2,
    len_ref, par_ref, ss, rs, ls, here,
):
    ctx, hx = lax.axis_index("ctx"), lax.axis_index("hx")
    x, z = lax.div(ctx, 8), lax.rem(ctx, 8)
    y, k = lax.div(hx, 2), lax.rem(hx, 2)
    chip = ctx * 4 + y

    def dev(dx=0, dy=0, dz=0, dk=0):
        xx, yy = lax.rem(x + dx, 4), lax.rem(y + dy, 4)
        zz, kk = lax.rem(z + dz, 8), lax.rem(k + dk, 2)
        return (xx * 8 + zz, yy * 2 + kk)

    count = [0, 0]
    sends = []

    def remote(src, dst, where):
        i = count[0]
        count[0] += 1
        copy = pltpu.make_async_remote_copy(
            src_ref=src, dst_ref=dst, send_sem=ss.at[i], recv_sem=rs.at[i],
            device_id=where, device_id_type=MESH,
        )
        copy.start()
        sends.append(copy)
        return copy

    def local(src, dst):
        i = count[1]
        count[1] += 1
        copy = pltpu.make_async_copy(src, dst, ls.at[i])
        copy.start()
        return copy

    kk = 1 - k
    head_rows = pl.ds(pl.multiple_of(hx * 16, 16), 16)
    key_rows = pl.ds(pl.multiple_of(k * 512, 512), 512)
    suf_rows = pl.ds(pl.multiple_of(k * 128, 128), 128)
    uo_rows = pl.ds(pl.multiple_of(k * 64, 64), 64)
    unit_rows = pl.ds(pl.multiple_of(k * 128, 128), 128)
    sv, srv = (s0, s1), (sr0, sr1)

    def kv_pairs(r, core):
        rows = slice(DR * r, DR * r + DR)
        return (
            (ck_hbm.at[2 * core + r], kv.at[r, key_rows]),
            (sl_hbm.at[pl.ds(8 * core + 4 * r, 4)], sv[r].at[:, suf_rows]),
            (cr_hbm.at[2 * core + r], kr.at[r, rows, key_rows]),
            (sr_hbm.at[pl.ds(8 * core + 4 * r, 4)], srv[r].at[:, rows, suf_rows]),
        )

    w_pairs = (
        (wuv_hbm, wuv.at[k]),
        (wo_hbm, wo.at[uo_rows]),
        (wg_hbm, wg.at[unit_rows]),
        (wu_hbm, wu.at[unit_rows]),
        (wd_hbm, wd.at[unit_rows]),
    )

    HX = [(dy, dk) for dy in (1, 3, 2, 0) for dk in range(2) if dy or dk]
    XY = [(dx, dy) for dx in range(4) for dy in range(4) if dx or dy]
    XY.sort(key=lambda d: -min(d[0], 4 - d[0]) - min(d[1], 4 - d[1]))
    ZK = [(dz, dk) for dz in (4, 3, 5, 2, 6, 1, 7, 0) for dk in range(2) if dz or dk]

    barrier = pltpu.get_barrier_semaphore()
    near = [dev(dx=1), dev(dx=3), dev(dz=1), dev(dz=7)]
    peers = [dev(dy=dy, dk=dk) for dy, dk in HX] + near
    for peer in peers:
        pl.semaphore_signal(barrier, inc=1, device_id=peer, device_id_type=MESH)
    own_q = [local(qr_hbm, rope)]
    own_q += [local(ql_hbm.at[pl.ds(8 * c, 4)], qc.at[c, :, :, :DL]) for c in range(2)]
    own = [[local(src, dst) for src, dst in kv_pairs(r, k)] for r in range(2)]
    own[0] += [local(len_hbm, len_ref), local(par_hbm, par_ref)]
    own[1].append(local(ql_hbm.at[pl.ds(8 * k + 4, 4)], qv1.at[:, head_rows]))
    own_w = [local(src, dst) for src, dst in w_pairs]
    small = [(hid_hbm, hid_ref), (gain_hbm, gain_ref), (ids_hbm, ids_ref), (gw_hbm, gw_ref)]
    own_small = [local(src, dst) for src, dst in small]
    kr[0, DR:] = jnp.zeros((DR, 1024), BF16)
    kr[1, :DR] = jnp.zeros((DR, 1024), BF16)
    sr0[:, DR:] = jnp.zeros((4, DR, 256), BF16)
    sr1[:, :DR] = jnp.zeros((4, DR, 256), BF16)
    own_q[0].wait()
    low = lax.broadcasted_iota(jnp.int32, (16, 128), 1) < DR
    for t in range(8):
        pair = rope[:, 128 * t : 128 * t + 128].astype(F32)
        swap = pltpu.roll(pair, DR, 1)
        ropes[pl.ds(2 * t, 16, stride=16), :] = jnp.where(low, pair, pltpu.roll(swap, 12, 0))
        ropes[pl.ds(2 * t + 1, 16, stride=16), :] = jnp.where(low, swap, pltpu.roll(pair, 12, 0))
    for c in range(2):
        for i in range(4):
            row = 16 * (8 * c + i)
            qc[c, i, :, DL:] = ropes[row : row + 16, :].astype(BF16)
    own_q[1].wait()
    own_q[2].wait()
    own[0].append(local(qc.at[k], qv0.at[:, head_rows]))
    pl.semaphore_wait(barrier, len(peers))

    def tell(i):
        for peer in near:
            pl.semaphore_signal(here.at[i], inc=1, device_id=peer, device_id_type=MESH)

    def hear(i):
        pl.semaphore_wait(here.at[i], len(near))

    beam = lax.rem(x + 2 * z, 4)
    got_q = {}
    for dy, dk in HX:
        core = lax.rem(k + dk, 2)
        if dy:
            src, dst = qc.at[core, beam], qv0.at[beam, head_rows]
        else:
            src, dst = qc.at[core], qv0.at[:, head_rows]
        got_q[dy, dk] = remote(src, dst, dev(dy=dy, dk=dk))
    tell(0)
    got_in = [[got_q[0, 1]], []]
    for src, dst in kv_pairs(0, kk):
        got_in[0].append(remote(src, dst, dev(dk=1)))
    for dy in (1, 3, 2):
        for copy in (got_q[dy, 0], got_q[dy, 1]):
            copy.wait_recv()
        rows = pl.ds(pl.multiple_of(lax.rem(y + 4 - dy, 4) * 32, 32), 32)
        block = qv0.at[beam, rows]
        for where in (dev(dx=1), dev(dx=3), dev(dz=1)):
            got_in[0].append(remote(block, block, where))

    hear(0)
    tell(1)
    for dy, dk in HX:
        core = lax.rem(k + dk, 2)
        src = ql_hbm.at[pl.ds(8 * core + 4, 4)]
        got_in[1].append(remote(src, qv1.at[:, head_rows], dev(dy=dy, dk=dk)))
    for src, dst in kv_pairs(1, kk):
        got_in[1].append(remote(src, dst, dev(dk=1)))
    def attend(r):
        for copy in own[r]:
            copy.wait()
        for copy in got_in[r]:
            copy.wait_recv()
        q = qv0[..., :DL] if r == 0 else qv1[...]
        qr = qv0[..., DL:]
        ql = q.reshape(4 * HEADS, DL)
        s = lax.dot_general(ql, kv[r], NT, preferred_element_type=F32)
        s = s + jnp.dot(
            qr.reshape(4 * HEADS, 128), kr[r], preferred_element_type=F32
        )
        pos = chip * 1024 + lax.broadcasted_iota(jnp.int32, (1, 1024), 1)
        s = jnp.where(pos < len_ref[2 * k + r], s * SCALE, NEG)
        high = jnp.max(s, axis=1, keepdims=True)
        rows = [slice(i * HEADS, (i + 1) * HEADS) for i in range(4)]
        own_s, tops, parent = [], [], []
        for i in range(4):
            p = lax.rem(par_ref[8 * k + 4 * r + i], 4)
            si = lax.dot_general(q[i], sv[r][p], NT, preferred_element_type=F32)
            si = si + jnp.dot(qr[i], srv[r][p], preferred_element_type=F32)
            own_s.append(si * SCALE)
            tops.append(jnp.maximum(high[rows[i]], jnp.max(own_s[i], axis=1, keepdims=True)))
            parent.append(p)
        w = jnp.exp2(s - jnp.concatenate(tops, axis=0)).astype(BF16)
        total = jnp.sum(w.astype(F32), axis=1, keepdims=True)
        acc = jnp.dot(w, kv[r], preferred_element_type=F32)
        totals = []
        for i in range(4):
            wi = jnp.exp2(own_s[i] - tops[i]).astype(BF16)
            totals.append(total[rows[i]] + jnp.sum(wi.astype(F32), axis=1, keepdims=True))
            ai = acc[rows[i]] + jnp.dot(wi, sv[r][parent[i]], preferred_element_type=F32)
            for l in range(4):
                tmp[i, l] = ai[:, 128 * l : 128 * l + 128]
        st[...] = stat_lanes(tops + totals, HEADS)
        for to in range(16):
            pick = pl.ds(32 * (to // 4) + to % 4, 8, stride=4)
            for l in range(4):
                block = jnp.concatenate([tmp[i, l, pick, :] for i in range(4)], axis=0)
                ob[r, to, :, 128 * l : 128 * l + 128] = block.astype(BF16)
            osb[r, to] = st[pick, :]

    me = x * 4 + y

    def join_send(r):
        got = []
        for j, (dx, dy) in enumerate(XY):
            to = lax.rem(x + dx, 4) * 4 + lax.rem(y + dy, 4)
            got.append(remote(osb.at[r, to], bsr.at[r, j], dev(dx=dx, dy=dy)))
            got.append(remote(ob.at[r, to], br.at[r, j], dev(dx=dx, dy=dy)))
        return got

    def join(r, got):
        for copy in got:
            copy.wait_recv()
        stats = [osb[r, me]] + [bsr[r, j] for j in range(15)]
        top = functools.reduce(jnp.maximum, stats)
        factors = [jnp.exp2(stat - top) for stat in stats]
        total = sum(pltpu.roll(f, 4, 1) * stat for f, stat in zip(factors, stats))
        for i in range(4):
            acc = jnp.zeros((8, DL), F32)
            for j in range(16):
                block = ob[r, me] if j == 0 else br[r, j - 1]
                rows = block.astype(F32)[8 * i : 8 * i + 8]
                acc = acc + rows * factors[j][:, i : i + 1]
            at = pl.ds((4 * r + i) * 8, 8)
            for l in range(4):
                zt[l, at] = acc[:, 128 * l : 128 * l + 128]
            zt[4, at] = stat_lanes([top[:, i : i + 1], total[:, 4 + i : 5 + i]], 8)

    hear(1)
    tell(2)
    attend(0)
    hear(2)
    tell(3)
    got_b0 = join_send(0)
    got_w = [remote(src, dst, dev(dk=1)) for src, dst in w_pairs]
    attend(1)
    hear(3)
    got_b1 = join_send(1)
    join(0, got_b0)
    join(1, got_b1)
    for b in range(8):
        for l in range(5):
            zsb[b, :, 128 * l : 128 * l + 128] = zt[l, pl.ds(b, 8, stride=8), :]
    got = []
    for dz in (4, 3, 5, 2, 6, 1, 7):
        got.append(remote(zsb.at[lax.rem(z + dz, 8)], zr.at[dz - 1], dev(dz=dz)))
    for copy in got:
        copy.wait_recv()
    parts = []
    for a in [zsb[z]] + [zr[j] for j in range(7)]:
        parts.append((a[:, DL : DL + 1], a[:, DL + 1 : DL + 2], a[:, :DL]))
    top, total, acc = fold(parts)
    attention = (acc / total).astype(BF16)

    for copy in own_w[:2]:
        copy.wait()
    for copy in got_w[:2]:
        copy.wait_recv()
    v0 = lax.dot_general(attention, wuv[0], NT, preferred_element_type=F32).astype(BF16)
    v1 = lax.dot_general(attention, wuv[1], NT, preferred_element_type=F32).astype(BF16)
    got = []
    for dz in (4, 3, 5, 2, 6, 1, 7, 0):
        b = lax.rem(z + dz, 8)
        cols = pl.ds(pl.multiple_of(b * 896, 128), 896)
        term = jnp.dot(v0, wo[:64, cols], preferred_element_type=F32)
        term = term + jnp.dot(v1, wo[64:, cols], preferred_element_type=F32)
        csb[b] = pack896(term).astype(BF16)
        if dz:
            got.append(remote(csb.at[b], cr1.at[dz - 1], dev(dz=dz)))
    for copy in got:
        copy.wait_recv()
    part = csb[z].astype(F32)
    for j in range(7):
        part = part + cr1[j].astype(F32)
    c2[me] = part.astype(BF16)
    got = []
    for dx, dy in XY:
        got.append(remote(c2.at[me], c2.at[me], dev(dx=dx, dy=dy)))
    for copy in got:
        copy.wait_recv()
    part = c2[0].astype(F32)
    for j in range(1, 16):
        part = part + c2[j].astype(F32)
    c3[z] = part.astype(BF16)
    got = []
    for dz in (4, 3, 5, 2, 6, 1, 7):
        got.append(remote(c3.at[z], c3.at[z], dev(dz=dz)))
    for copy in got:
        copy.wait_recv()
    got_att = remote(c3, c3o, dev(dk=1))

    for copy in own_small:
        copy.wait()
    square = jnp.zeros((8, 1), F32)
    for b in range(8):
        block = c3[b].astype(F32)
        for half, width in ((0, 512), (1, 384)):
            cols = slice(896 * b + 512 * half, 896 * b + 512 * half + width)
            hid = hid_ref[:, cols].astype(F32)
            hid = jnp.where(k == 0, hid[:8], hid[8:])
            value = hid + block[8 * half : 8 * half + 8, :width]
            res[:, cols] = value
            square = square + jnp.sum(value * value, axis=1, keepdims=True)
    scale = lax.rsqrt(square / D + 1e-6)
    nrm[...] = (res[...] * scale * gain_ref[...]).astype(BF16)

    expert = lax.div(ctx, 2)
    route = jnp.sum(gw_ref[...] * (ids_ref[...] == expert).astype(F32), axis=0, keepdims=True)
    row = lax.broadcasted_iota(jnp.int32, (8, HYPS), 0)
    col = lax.broadcasted_iota(jnp.int32, (8, HYPS), 1)
    route = jnp.sum(jnp.where(col == row + 8 * k, route, 0.0), axis=1, keepdims=True)
    for copy in own_w[2:]:
        copy.wait()
    for copy in got_w[2:]:
        copy.wait_recv()
    gate = lax.dot_general(nrm[...], wg[...], NT, preferred_element_type=F32)
    up = lax.dot_general(nrm[...], wu[...], NT, preferred_element_type=F32)
    act = (gate / (1.0 + jnp.exp(-gate)) * up * route).astype(BF16)
    start = x * 1792 + z * 224 + y * 56
    lane = lax.broadcasted_iota(jnp.int32, (8, 128), 1)
    got = []
    for dx in (2, 1, 3, 0):
        b = lax.rem(x + dx, 4)
        tiles = []
        for t in range(14):
            at = b * 1792 + 128 * t
            if t % 7 == 0:
                wide = pl.ds(pl.multiple_of(at, 128), 896)
                term = jnp.dot(act, wd[:, wide], preferred_element_type=F32)
            piece = term[:, 128 * (t % 7) : 128 * (t % 7) + 128]
            if dx == 0:
                col = lane + at
                mine = (col >= start) & (col < start + 56)
                rest = res[:, pl.ds(pl.multiple_of(at, 128), 128)]
                piece = piece + jnp.where(mine, rest, 0.0)
            tiles.append(piece)
        for c in range(4):
            halves = [
                jnp.where(
                    lane < 64,
                    window(tiles, 448 * u + 56 * c, 0),
                    window(tiles, 448 * u + 224 + 56 * c, 64),
                )
                for u in range(4)
            ]
            whole = jnp.concatenate(halves, axis=1)
            if dx == 0:
                e1f[c] = whole
            esb[4 * b + c] = jnp.concatenate([whole[:, :256], whole[:, 256:]], axis=0).astype(BF16)
        for dy in (2, 1, 3, 0):
            if dx or dy:
                to = 4 * b + lax.rem(y + dy, 4)
                got.append(remote(esb.at[to], er1.at[4 * dx + dy - 1], dev(dx=dx, dy=dy)))
    got_att.wait_recv()
    for b in range(8):
        a, o = c3[b].astype(F32), c3o[b].astype(F32)
        first, second = jnp.where(k == 0, a, o), jnp.where(k == 0, o, a)
        for half, width in ((0, 512), (1, 384)):
            cols = slice(896 * b + 512 * half, 896 * b + 512 * half + width)
            rows = slice(8 * half, 8 * half + 8)
            pair = jnp.concatenate([first[rows, :width], second[rows, :width]], axis=0)
            att_ref[:, cols] = pair.astype(BF16)
    for copy in got:
        copy.wait_recv()
    part = er1[0].astype(F32)
    for j in range(1, 15):
        part = part + er1[j].astype(F32)
    part = jnp.concatenate([part[:8], part[8:]], axis=1) + e1f[y]
    for b in range(8):
        tile = part[:, 128 * (b // 2) : 128 * (b // 2) + 128]
        for c in range(2):
            off = 64 * (b % 2) + 28 * c
            e2b[2 * b + c] = pltpu.roll(tile, 128 - off, 1) if off else tile
    got = []
    for j, (dz, dk) in enumerate(ZK):
        to = lax.rem(z + dz, 8) * 2 + lax.rem(k + dk, 2)
        got.append(remote(e2b.at[to], er2.at[j], dev(dz=dz, dk=dk)))
    for copy in got:
        copy.wait_recv()
    same, other = e2b[2 * z + k], jnp.zeros((8, 128), F32)
    for j, (dz, dk) in enumerate(ZK):
        if dk:
            other = other + er2[j]
        else:
            same = same + er2[j]
    both = jnp.concatenate(
        [jnp.where(k == 0, same, other), jnp.where(k == 0, other, same)], axis=0
    )
    upd_ref[...] = both[:, :28].astype(BF16)

    for copy in sends:
        copy.wait_send()


def local(
    query_latent, query_rope, cache_latent, cache_rope, suffix_latent, suffix_rope, lengths,
    parents, w_uv, w_o, hidden, norm_gain, w_gate, w_up, w_down, expert_ids, gate_weights,
):
    hbm = pl.BlockSpec(memory_space=pltpu.HBM)
    vmem = pl.BlockSpec(memory_space=pltpu.VMEM)
    scratch = [
        ((HYPS, D), BF16),
        ((1, D), F32),
        ((8, HYPS), jnp.int32),
        ((8, HYPS), F32),
        ((HYPS, 16 * DR), BF16),
        ((256, 128), F32),
        ((2, 4, 16, DL + 128), BF16),
        ((4, 128, DL + 128), BF16),
        ((4, 128, DL), BF16),
        ((2, 1024, DL), BF16),
        ((2, 2 * DR, 1024), BF16),
        ((4, 256, DL), BF16),
        ((4, 256, DL), BF16),
        ((4, 2 * DR, 256), BF16),
        ((4, 2 * DR, 256), BF16),
        ((2, 64, DL), BF16),
        ((128, D), BF16),
        ((256, D), BF16),
        ((256, D), BF16),
        ((256, D), BF16),
        ((4, 4, HEADS, 128), F32),
        ((HEADS, 128), F32),
        ((2, 16, 32, DL), BF16),
        ((2, 16, 8, 128), F32),
        ((2, 15, 32, DL), BF16),
        ((2, 15, 8, 128), F32),
        ((5, 64, 128), F32),
        ((8, 8, 640), F32),
        ((7, 8, 640), F32),
        ((8, 16, 512), BF16),
        ((7, 16, 512), BF16),
        ((16, 16, 512), BF16),
        ((8, 16, 512), BF16),
        ((8, 16, 512), BF16),
        ((8, D), F32),
        ((8, D), BF16),
        ((4, 8, 512), F32),
        ((16, 16, 256), BF16),
        ((15, 16, 256), BF16),
        ((16, 8, 128), F32),
        ((15, 8, 128), F32),
    ]
    return pl.pallas_call(
        kernel,
        name="decode_step",
        out_shape=(
            jax.ShapeDtypeStruct((HYPS, D), BF16),
            jax.ShapeDtypeStruct((HYPS, 28), BF16),
        ),
        in_specs=[hbm] * 17,
        out_specs=(vmem, vmem),
        scratch_shapes=[pltpu.VMEM(shape, dtype) for shape, dtype in scratch]
        + [
            pltpu.SMEM((4,), jnp.int32),
            pltpu.SMEM((16,), jnp.int32),
            pltpu.SemaphoreType.DMA((N_SEMS,)),
            pltpu.SemaphoreType.DMA((N_SEMS,)),
            pltpu.SemaphoreType.DMA((N_LOCAL,)),
            pltpu.SemaphoreType.REGULAR((4,)),
        ],
        compiler_params=pltpu.CompilerParams(
            collective_id=0, has_side_effects=True, vmem_limit_bytes=48 << 20
        ),
    )(
        *(
            pltpu.with_memory_space_constraint(value, pltpu.HBM)
            for value in (
                query_latent, query_rope, cache_latent, cache_rope, suffix_latent, suffix_rope,
                w_uv.T, w_o, w_gate, w_up, w_down, lengths, parents, hidden,
                norm_gain.reshape(1, D), expert_ids.T, gate_weights.T,
            )
        )
    )


def solution(mesh):
    both = ("ctx", "hx")
    in_specs = (
        P(None, "hx", None),
        P(None, "hx"),
        P(None, both, None),
        P(None, None, both),
        P(None, both, None),
        P(None, None, both),
        P(),
        P(),
        P(None, both),
        P(both, None),
        P(),
        P(),
        P(both, None),
        P(both, None),
        P(both, None),
        P(),
        P(),
    )
    out_specs = (P(), P(None, both))
    return jax.shard_map(local, mesh=mesh, in_specs=in_specs, out_specs=out_specs, check_vma=False)
```

```python
import functools
import math

import jax
import jax.numpy as jnp
from jax import lax
from jax.experimental import pallas as pl
from jax.experimental.pallas import tpu as pltpu
from jax.sharding import PartitionSpec as P

MESH = pl.DeviceIdType.MESH
F32 = jnp.float32
BF16 = jnp.bfloat16

DL = 512
DR = 64
DN = 128
D = 7168
HYPS = 16
HEADS = 128
MSCALE = 1.0 + 0.1 * math.log(40.0)
SCALE = MSCALE * MSCALE / math.sqrt(DN + DR) * math.log2(math.e)
NEG = -1e30
NT = (((1,), (1,)), ((), ()))

N_SEMS = 184
N_LOCAL = 24


def fold(parts):
    top = functools.reduce(jnp.maximum, [p[0] for p in parts])
    total, acc = 0.0, 0.0
    for high, tot, sums in parts:
        factor = jnp.exp2(high - top)
        total = total + tot * factor
        acc = acc + sums * factor
    return top, total, acc


def stat_lanes(columns, rows):
    lane = lax.broadcasted_iota(jnp.int32, (rows, 128), 1)
    out = jnp.zeros((rows, 128), F32)
    for j, column in enumerate(columns):
        out = jnp.where(lane == j, column, out)
    return out


def window(tiles, start, dest):
    at, off = divmod(start, 128)
    shift = (dest - off) % 128
    out = pltpu.roll(tiles[at], shift, 1) if shift else tiles[at]
    if off + 56 > 128:
        lane = lax.broadcasted_iota(jnp.int32, (8, 128), 1)
        after = pltpu.roll(tiles[at + 1], shift, 1) if shift else tiles[at + 1]
        out = jnp.where(lane < dest + 128 - off, out, after)
    return out


def pack896(part):
    low = jnp.concatenate([part[:, 512:], jnp.zeros((8, 128), part.dtype)], axis=1)
    return jnp.concatenate([part[:, :512], low], axis=0)


def kernel(
    ql_hbm, qr_hbm, ck_hbm, cr_hbm, sl_hbm, sr_hbm, wuv_hbm, wo_hbm, wg_hbm, wu_hbm, wd_hbm,
    len_hbm, par_hbm, hid_hbm, gain_hbm, ids_hbm, gw_hbm,
    att_ref, upd_ref,
    hid_ref, gain_ref, ids_ref, gw_ref, rope, ropes, qc, qv0, qv1, kv, kr, s0, s1, sr0, sr1,
    wuv, wo, wg, wu, wd, tmp, st, ob, osb, br, bsr, zt, zsb, zr,
    csb, cr1, c2, c3, c3o, res, nrm, e1f, esb, er1, e2b, er2,
    len_ref, par_ref, ss, rs, ls, here,
):
    ctx, hx = lax.axis_index("ctx"), lax.axis_index("hx")
    x, z = lax.div(ctx, 8), lax.rem(ctx, 8)
    y, k = lax.div(hx, 2), lax.rem(hx, 2)
    chip = ctx * 4 + y

    def dev(dx=0, dy=0, dz=0, dk=0):
        xx, yy = lax.rem(x + dx, 4), lax.rem(y + dy, 4)
        zz, kk = lax.rem(z + dz, 8), lax.rem(k + dk, 2)
        return (xx * 8 + zz, yy * 2 + kk)

    count = [0, 0]
    sends = []

    def remote(src, dst, where):
        i = count[0]
        count[0] += 1
        copy = pltpu.make_async_remote_copy(
            src_ref=src, dst_ref=dst, send_sem=ss.at[i], recv_sem=rs.at[i],
            device_id=where, device_id_type=MESH,
        )
        copy.start()
        sends.append(copy)
        return copy

    def local(src, dst):
        i = count[1]
        count[1] += 1
        copy = pltpu.make_async_copy(src, dst, ls.at[i])
        copy.start()
        return copy

    kk = 1 - k
    head_rows = pl.ds(pl.multiple_of(hx * 16, 16), 16)
    key_rows = pl.ds(pl.multiple_of(k * 512, 512), 512)
    suf_rows = pl.ds(pl.multiple_of(k * 128, 128), 128)
    uo_rows = pl.ds(pl.multiple_of(k * 64, 64), 64)
    unit_rows = pl.ds(pl.multiple_of(k * 128, 128), 128)
    sv, srv = (s0, s1), (sr0, sr1)

    def kv_pairs(r, core):
        rows = slice(DR * r, DR * r + DR)
        return (
            (ck_hbm.at[2 * core + r], kv.at[r, key_rows]),
            (sl_hbm.at[pl.ds(8 * core + 4 * r, 4)], sv[r].at[:, suf_rows]),
            (cr_hbm.at[2 * core + r], kr.at[r, rows, key_rows]),
            (sr_hbm.at[pl.ds(8 * core + 4 * r, 4)], srv[r].at[:, rows, suf_rows]),
        )

    w_pairs = (
        (wuv_hbm, wuv.at[k]),
        (wo_hbm, wo.at[uo_rows]),
        (wg_hbm, wg.at[unit_rows]),
        (wu_hbm, wu.at[unit_rows]),
        (wd_hbm, wd.at[unit_rows]),
    )

    HX = [(dy, dk) for dy in (2, 1, 3, 0) for dk in range(2) if dy or dk]
    XY = [(dx, dy) for dx in range(4) for dy in range(4) if dx or dy]
    XY.sort(key=lambda d: -min(d[0], 4 - d[0]) - min(d[1], 4 - d[1]))
    ZK = [(dz, dk) for dz in (4, 3, 5, 2, 6, 1, 7, 0) for dk in range(2) if dz or dk]

    barrier = pltpu.get_barrier_semaphore()
    near = [dev(dx=1), dev(dx=3), dev(dz=1), dev(dz=7)]
    peers = [dev(dy=dy, dk=dk) for dy, dk in HX] + near
    for peer in peers:
        pl.semaphore_signal(barrier, inc=1, device_id=peer, device_id_type=MESH)
    own_q = [local(qr_hbm, rope)]
    own_q += [local(ql_hbm.at[pl.ds(8 * c, 4)], qc.at[c, :, :, :DL]) for c in range(2)]
    own = [[local(src, dst) for src, dst in kv_pairs(r, k)] for r in range(2)]
    own[0] += [local(len_hbm, len_ref), local(par_hbm, par_ref)]
    own[1].append(local(ql_hbm.at[pl.ds(8 * k + 4, 4)], qv1.at[:, head_rows]))
    own_w = [local(src, dst) for src, dst in w_pairs]
    small = [(hid_hbm, hid_ref), (gain_hbm, gain_ref), (ids_hbm, ids_ref), (gw_hbm, gw_ref)]
    own_small = [local(src, dst) for src, dst in small]
    kr[0, DR:] = jnp.zeros((DR, 1024), BF16)
    kr[1, :DR] = jnp.zeros((DR, 1024), BF16)
    sr0[:, DR:] = jnp.zeros((4, DR, 256), BF16)
    sr1[:, :DR] = jnp.zeros((4, DR, 256), BF16)
    own_q[0].wait()
    low = lax.broadcasted_iota(jnp.int32, (16, 128), 1) < DR
    for t in range(8):
        pair = rope[:, 128 * t : 128 * t + 128].astype(F32)
        swap = pltpu.roll(pair, DR, 1)
        ropes[pl.ds(2 * t, 16, stride=16), :] = jnp.where(low, pair, pltpu.roll(swap, 12, 0))
        ropes[pl.ds(2 * t + 1, 16, stride=16), :] = jnp.where(low, swap, pltpu.roll(pair, 12, 0))
    for c in range(2):
        for i in range(4):
            row = 16 * (8 * c + i)
            qc[c, i, :, DL:] = ropes[row : row + 16, :].astype(BF16)
    own_q[1].wait()
    own_q[2].wait()
    own[0].append(local(qc.at[k], qv0.at[:, head_rows]))
    pl.semaphore_wait(barrier, len(peers))

    def tell(i):
        for peer in near:
            pl.semaphore_signal(here.at[i], inc=1, device_id=peer, device_id_type=MESH)

    def hear(i):
        pl.semaphore_wait(here.at[i], len(near))

    beam = lax.rem(x + 2 * z, 4)
    got_q = {}
    for dy, dk in HX:
        core = lax.rem(k + dk, 2)
        if dy:
            src, dst = qc.at[core, beam], qv0.at[beam, head_rows]
        else:
            src, dst = qc.at[core], qv0.at[:, head_rows]
        got_q[dy, dk] = remote(src, dst, dev(dy=dy, dk=dk))
    tell(0)
    got_in = [[got_q[0, 1]], []]
    for src, dst in kv_pairs(0, kk):
        got_in[0].append(remote(src, dst, dev(dk=1)))
    for dy in (1, 3, 2):
        for copy in (got_q[dy, 0], got_q[dy, 1]):
            copy.wait_recv()
        rows = pl.ds(pl.multiple_of(lax.rem(y + 4 - dy, 4) * 32, 32), 32)
        block = qv0.at[beam, rows]
        for where in (dev(dx=1), dev(dx=3), dev(dz=1)):
            got_in[0].append(remote(block, block, where))

    hear(0)
    tell(1)
    for dy, dk in HX:
        core = lax.rem(k + dk, 2)
        src = ql_hbm.at[pl.ds(8 * core + 4, 4)]
        got_in[1].append(remote(src, qv1.at[:, head_rows], dev(dy=dy, dk=dk)))
    for src, dst in kv_pairs(1, kk):
        got_in[1].append(remote(src, dst, dev(dk=1)))
    def attend(r, beams):
        few = len(beams)
        first = beams[0]
        q = (qv1 if r else qv0)[first : first + few, :, :DL]
        qr = qv0[first : first + few, :, DL:]
        s = lax.dot_general(q.reshape(few * HEADS, DL), kv[r], NT, preferred_element_type=F32)
        s = s + jnp.dot(qr.reshape(few * HEADS, 128), kr[r], preferred_element_type=F32)
        pos = chip * 1024 + lax.broadcasted_iota(jnp.int32, (1, 1024), 1)
        s = jnp.where(pos < len_ref[2 * k + r], s * SCALE, NEG)
        high = jnp.max(s, axis=1, keepdims=True)
        rows = [slice(i * HEADS, (i + 1) * HEADS) for i in range(few)]
        own_s, tops, parent = [], [], []
        for i in range(few):
            p = lax.rem(par_ref[8 * k + 4 * r + first + i], 4)
            si = lax.dot_general(q[i], sv[r][p], NT, preferred_element_type=F32)
            si = si + jnp.dot(qr[i], srv[r][p], preferred_element_type=F32)
            own_s.append(si * SCALE)
            tops.append(jnp.maximum(high[rows[i]], jnp.max(own_s[i], axis=1, keepdims=True)))
            parent.append(p)
        w = jnp.exp2(s - jnp.concatenate(tops, axis=0)).astype(BF16)
        total = jnp.sum(w.astype(F32), axis=1, keepdims=True)
        acc = jnp.dot(w, kv[r], preferred_element_type=F32)
        totals = []
        for i in range(few):
            wi = jnp.exp2(own_s[i] - tops[i]).astype(BF16)
            totals.append(total[rows[i]] + jnp.sum(wi.astype(F32), axis=1, keepdims=True))
            ai = acc[rows[i]] + jnp.dot(wi, sv[r][parent[i]], preferred_element_type=F32)
            for l in range(4):
                tmp[i, l] = ai[:, 128 * l : 128 * l + 128]
        none = [0.0] * first
        rest = [0.0] * (4 - few - first)
        lane = lax.broadcasted_iota(jnp.int32, (HEADS, 128), 1)
        row = lax.broadcasted_iota(jnp.int32, (HEADS, 128), 0)
        lane = lane - 8 * jnp.bitwise_and(jnp.right_shift(row, 2), 7)
        stat = jnp.zeros((HEADS, 128), F32)
        for j, figure in enumerate(none + tops + rest + none + totals + rest):
            if not isinstance(figure, float):
                stat = jnp.where(lane == j, figure, stat)
        st[...] = st[...] + stat if first else stat
        for to in range(16):
            pick = pl.ds(32 * (to // 4) + to % 4, 8, stride=4)
            for l in range(4):
                block = jnp.concatenate([tmp[i, l, pick, :] for i in range(few)], axis=0)
                lanes = slice(128 * l, 128 * l + 128)
                ob[r, to, 8 * first : 8 * (first + few), lanes] = block.astype(BF16)
            if first + few == 4:
                osb[r, to] = jnp.sum(st[pick, :], axis=0, keepdims=True)

    me = x * 4 + y

    def join_send(r, beams):
        got = []
        rows = pl.ds(8 * beams[0], 8 * len(beams))
        for j, (dx, dy) in enumerate(XY):
            to = lax.rem(x + dx, 4) * 4 + lax.rem(y + dy, 4)
            if beams[-1] == 3:
                got.append(remote(osb.at[r, to], bsr.at[r, j], dev(dx=dx, dy=dy)))
            got.append(remote(ob.at[r, to, rows], br.at[r, j, rows], dev(dx=dx, dy=dy)))
        return got

    def join(r, got):
        for copy in got:
            copy.wait_recv()
        lane = lax.broadcasted_iota(jnp.int32, (8, 128), 1)
        lane = lane - 8 * lax.broadcasted_iota(jnp.int32, (8, 128), 0)

        def column(figures, j):
            return jnp.sum(jnp.where(lane == j, figures, 0.0), axis=1, keepdims=True)

        stats = [osb[r, me]] + [bsr[r, j] for j in range(15)]
        top = functools.reduce(jnp.maximum, stats)
        factors = [jnp.exp2(stat - top) for stat in stats]
        total = sum(pltpu.roll(f, 4, 1) * stat for f, stat in zip(factors, stats))
        for i in range(4):
            acc = jnp.zeros((8, DL), F32)
            for j in range(16):
                block = ob[r, me] if j == 0 else br[r, j - 1]
                rows = block.astype(F32)[8 * i : 8 * i + 8]
                acc = acc + rows * column(factors[j], i)
            at = pl.ds((4 * r + i) * 8, 8)
            for l in range(4):
                zt[l, at] = acc[:, 128 * l : 128 * l + 128]
            zt[4, at] = stat_lanes([column(top, i), column(total, 4 + i)], 8)

    hear(1)
    tell(2)
    for copy in own[0]:
        copy.wait()
    for copy in got_in[0]:
        copy.wait_recv()
    attend(0, [0, 1])
    got_b0 = join_send(0, [0, 1])
    attend(0, [2, 3])
    hear(2)
    tell(3)
    got_b0 += join_send(0, [2, 3])
    got_w = [remote(src, dst, dev(dk=1)) for src, dst in w_pairs]
    for copy in own[1]:
        copy.wait()
    for copy in got_in[1]:
        copy.wait_recv()
    attend(1, [0, 1, 2, 3])
    hear(3)
    got_b1 = join_send(1, [0, 1, 2, 3])
    join(0, got_b0)
    join(1, got_b1)
    for b in range(8):
        for l in range(5):
            zsb[b, :, 128 * l : 128 * l + 128] = zt[l, pl.ds(b, 8, stride=8), :]
    got = []
    for dz in (4, 3, 5, 2, 6, 1, 7):
        got.append(remote(zsb.at[lax.rem(z + dz, 8)], zr.at[dz - 1], dev(dz=dz)))
    for copy in got:
        copy.wait_recv()
    parts = []
    for a in [zsb[z]] + [zr[j] for j in range(7)]:
        parts.append((a[:, DL : DL + 1], a[:, DL + 1 : DL + 2], a[:, :DL]))
    top, total, acc = fold(parts)
    attention = (acc / total).astype(BF16)

    for copy in own_w[:2]:
        copy.wait()
    for copy in got_w[:2]:
        copy.wait_recv()
    v0 = lax.dot_general(attention, wuv[0], NT, preferred_element_type=F32).astype(BF16)
    v1 = lax.dot_general(attention, wuv[1], NT, preferred_element_type=F32).astype(BF16)
    got = []
    for dz in (4, 3, 5, 2, 6, 1, 7, 0):
        b = lax.rem(z + dz, 8)
        cols = pl.ds(pl.multiple_of(b * 896, 128), 896)
        term = jnp.dot(v0, wo[:64, cols], preferred_element_type=F32)
        term = term + jnp.dot(v1, wo[64:, cols], preferred_element_type=F32)
        csb[b] = pack896(term).astype(BF16)
        if dz:
            got.append(remote(csb.at[b], cr1.at[dz - 1], dev(dz=dz)))
    for copy in got:
        copy.wait_recv()
    part = csb[z].astype(F32)
    for j in range(7):
        part = part + cr1[j].astype(F32)
    c2[me] = part.astype(BF16)
    got = []
    for dx, dy in XY:
        got.append(remote(c2.at[me], c2.at[me], dev(dx=dx, dy=dy)))
    for copy in got:
        copy.wait_recv()
    part = c2[0].astype(F32)
    for j in range(1, 16):
        part = part + c2[j].astype(F32)
    c3[z] = part.astype(BF16)
    got = []
    for dz in (4, 3, 5, 2, 6, 1, 7):
        got.append(remote(c3.at[z], c3.at[z], dev(dz=dz)))
    for copy in got:
        copy.wait_recv()
    got_att = remote(c3, c3o, dev(dk=1))

    for copy in own_small:
        copy.wait()
    square = jnp.zeros((8, 1), F32)
    for b in range(8):
        block = c3[b].astype(F32)
        for half, width in ((0, 512), (1, 384)):
            cols = slice(896 * b + 512 * half, 896 * b + 512 * half + width)
            hid = hid_ref[:, cols].astype(F32)
            hid = jnp.where(k == 0, hid[:8], hid[8:])
            value = hid + block[8 * half : 8 * half + 8, :width]
            res[:, cols] = value
            square = square + jnp.sum(value * value, axis=1, keepdims=True)
    scale = lax.rsqrt(square / D + 1e-6)
    nrm[...] = (res[...] * scale * gain_ref[...]).astype(BF16)

    expert = lax.div(ctx, 2)
    route = jnp.sum(gw_ref[...] * (ids_ref[...] == expert).astype(F32), axis=0, keepdims=True)
    row = lax.broadcasted_iota(jnp.int32, (8, HYPS), 0)
    col = lax.broadcasted_iota(jnp.int32, (8, HYPS), 1)
    route = jnp.sum(jnp.where(col == row + 8 * k, route, 0.0), axis=1, keepdims=True)
    for copy in own_w[2:]:
        copy.wait()
    for copy in got_w[2:]:
        copy.wait_recv()
    gate = lax.dot_general(nrm[...], wg[...], NT, preferred_element_type=F32)
    up = lax.dot_general(nrm[...], wu[...], NT, preferred_element_type=F32)
    act = (gate / (1.0 + jnp.exp(-gate)) * up * route).astype(BF16)
    start = x * 1792 + z * 224 + y * 56
    lane = lax.broadcasted_iota(jnp.int32, (8, 128), 1)
    got = []
    for dx in (2, 1, 3, 0):
        b = lax.rem(x + dx, 4)
        tiles = []
        for t in range(14):
            at = b * 1792 + 128 * t
            if t % 7 == 0:
                wide = pl.ds(pl.multiple_of(at, 128), 896)
                term = jnp.dot(act, wd[:, wide], preferred_element_type=F32)
            piece = term[:, 128 * (t % 7) : 128 * (t % 7) + 128]
            if dx == 0:
                col = lane + at
                mine = (col >= start) & (col < start + 56)
                rest = res[:, pl.ds(pl.multiple_of(at, 128), 128)]
                piece = piece + jnp.where(mine, rest, 0.0)
            tiles.append(piece)
        for c in range(4):
            halves = [
                jnp.where(
                    lane < 64,
                    window(tiles, 448 * u + 56 * c, 0),
                    window(tiles, 448 * u + 224 + 56 * c, 64),
                )
                for u in range(4)
            ]
            whole = jnp.concatenate(halves, axis=1)
            if dx == 0:
                e1f[c] = whole
            esb[4 * b + c] = jnp.concatenate([whole[:, :256], whole[:, 256:]], axis=0).astype(BF16)
        for dy in (2, 1, 3, 0):
            if dx or dy:
                to = 4 * b + lax.rem(y + dy, 4)
                got.append(remote(esb.at[to], er1.at[4 * dx + dy - 1], dev(dx=dx, dy=dy)))
    got_att.wait_recv()
    for b in range(8):
        a, o = c3[b].astype(F32), c3o[b].astype(F32)
        first, second = jnp.where(k == 0, a, o), jnp.where(k == 0, o, a)
        for half, width in ((0, 512), (1, 384)):
            cols = slice(896 * b + 512 * half, 896 * b + 512 * half + width)
            rows = slice(8 * half, 8 * half + 8)
            pair = jnp.concatenate([first[rows, :width], second[rows, :width]], axis=0)
            att_ref[:, cols] = pair.astype(BF16)
    for copy in got:
        copy.wait_recv()
    part = er1[0].astype(F32)
    for j in range(1, 15):
        part = part + er1[j].astype(F32)
    part = jnp.concatenate([part[:8], part[8:]], axis=1) + e1f[y]
    for b in range(8):
        tile = part[:, 128 * (b // 2) : 128 * (b // 2) + 128]
        for c in range(2):
            off = 64 * (b % 2) + 28 * c
            e2b[2 * b + c] = pltpu.roll(tile, 128 - off, 1) if off else tile
    got = []
    for j, (dz, dk) in enumerate(ZK):
        to = lax.rem(z + dz, 8) * 2 + lax.rem(k + dk, 2)
        got.append(remote(e2b.at[to], er2.at[j], dev(dz=dz, dk=dk)))
    for copy in got:
        copy.wait_recv()
    same, other = e2b[2 * z + k], jnp.zeros((8, 128), F32)
    for j, (dz, dk) in enumerate(ZK):
        if dk:
            other = other + er2[j]
        else:
            same = same + er2[j]
    both = jnp.concatenate(
        [jnp.where(k == 0, same, other), jnp.where(k == 0, other, same)], axis=0
    )
    upd_ref[...] = both[:, :28].astype(BF16)

    for copy in sends:
        copy.wait_send()


def local(
    query_latent, query_rope, cache_latent, cache_rope, suffix_latent, suffix_rope, lengths,
    parents, w_uv, w_o, hidden, norm_gain, w_gate, w_up, w_down, expert_ids, gate_weights,
):
    hbm = pl.BlockSpec(memory_space=pltpu.HBM)
    vmem = pl.BlockSpec(memory_space=pltpu.VMEM)
    scratch = [
        ((HYPS, D), BF16),
        ((1, D), F32),
        ((8, HYPS), jnp.int32),
        ((8, HYPS), F32),
        ((HYPS, 16 * DR), BF16),
        ((256, 128), F32),
        ((2, 4, 16, DL + 128), BF16),
        ((4, 128, DL + 128), BF16),
        ((4, 128, DL), BF16),
        ((2, 1024, DL), BF16),
        ((2, 2 * DR, 1024), BF16),
        ((4, 256, DL), BF16),
        ((4, 256, DL), BF16),
        ((4, 2 * DR, 256), BF16),
        ((4, 2 * DR, 256), BF16),
        ((2, 64, DL), BF16),
        ((128, D), BF16),
        ((256, D), BF16),
        ((256, D), BF16),
        ((256, D), BF16),
        ((4, 4, HEADS, 128), F32),
        ((HEADS, 128), F32),
        ((2, 16, 32, DL), BF16),
        ((2, 16, 1, 128), F32),
        ((2, 15, 32, DL), BF16),
        ((2, 15, 1, 128), F32),
        ((5, 64, 128), F32),
        ((8, 8, 640), F32),
        ((7, 8, 640), F32),
        ((8, 16, 512), BF16),
        ((7, 16, 512), BF16),
        ((16, 16, 512), BF16),
        ((8, 16, 512), BF16),
        ((8, 16, 512), BF16),
        ((8, D), F32),
        ((8, D), BF16),
        ((4, 8, 512), F32),
        ((16, 16, 256), BF16),
        ((15, 16, 256), BF16),
        ((16, 8, 128), F32),
        ((15, 8, 128), F32),
    ]
    return pl.pallas_call(
        kernel,
        name="decode_step",
        out_shape=(
            jax.ShapeDtypeStruct((HYPS, D), BF16),
            jax.ShapeDtypeStruct((HYPS, 28), BF16),
        ),
        in_specs=[hbm] * 17,
        out_specs=(vmem, vmem),
        scratch_shapes=[pltpu.VMEM(shape, dtype) for shape, dtype in scratch]
        + [
            pltpu.SMEM((4,), jnp.int32),
            pltpu.SMEM((16,), jnp.int32),
            pltpu.SemaphoreType.DMA((N_SEMS,)),
            pltpu.SemaphoreType.DMA((N_SEMS,)),
            pltpu.SemaphoreType.DMA((N_LOCAL,)),
            pltpu.SemaphoreType.REGULAR((4,)),
        ],
        compiler_params=pltpu.CompilerParams(
            collective_id=0, has_side_effects=True, vmem_limit_bytes=48 << 20
        ),
    )(
        *(
            pltpu.with_memory_space_constraint(value, pltpu.HBM)
            for value in (
                query_latent, query_rope, cache_latent, cache_rope, suffix_latent, suffix_rope,
                w_uv.T, w_o, w_gate, w_up, w_down, lengths, parents, hidden,
                norm_gain.reshape(1, D), expert_ids.T, gate_weights.T,
            )
        )
    )


def solution(mesh):
    both = ("ctx", "hx")
    in_specs = (
        P(None, "hx", None),
        P(None, "hx"),
        P(None, both, None),
        P(None, None, both),
        P(None, both, None),
        P(None, None, both),
        P(),
        P(),
        P(None, both),
        P(both, None),
        P(),
        P(),
        P(both, None),
        P(both, None),
        P(both, None),
        P(),
        P(),
    )
    out_specs = (P(), P(None, both))
    return jax.shard_map(local, mesh=mesh, in_specs=in_specs, out_specs=out_specs, check_vma=False)
```

```python
import functools
import math

import jax
import jax.numpy as jnp
from jax import lax
from jax.experimental import pallas as pl
from jax.experimental.pallas import tpu as pltpu
from jax.sharding import PartitionSpec as P

MESH = pl.DeviceIdType.MESH
F32 = jnp.float32
BF16 = jnp.bfloat16

DL = 512
DR = 64
DN = 128
D = 7168
HYPS = 16
HEADS = 128
MSCALE = 1.0 + 0.1 * math.log(40.0)
SCALE = MSCALE * MSCALE / math.sqrt(DN + DR) * math.log2(math.e)
NEG = -1e30
NT = (((1,), (1,)), ((), ()))

N_SEMS = 192
N_LOCAL = 24


def fold(parts):
    top = functools.reduce(jnp.maximum, [p[0] for p in parts])
    total, acc = 0.0, 0.0
    for high, tot, sums in parts:
        factor = jnp.exp2(high - top)
        total = total + tot * factor
        acc = acc + sums * factor
    return top, total, acc


def stat_lanes(columns, rows):
    lane = lax.broadcasted_iota(jnp.int32, (rows, 128), 1)
    out = jnp.zeros((rows, 128), F32)
    for j, column in enumerate(columns):
        out = jnp.where(lane == j, column, out)
    return out


def window(tiles, start, dest):
    at, off = divmod(start, 128)
    shift = (dest - off) % 128
    out = pltpu.roll(tiles[at], shift, 1) if shift else tiles[at]
    if off + 56 > 128:
        lane = lax.broadcasted_iota(jnp.int32, (8, 128), 1)
        after = pltpu.roll(tiles[at + 1], shift, 1) if shift else tiles[at + 1]
        out = jnp.where(lane < dest + 128 - off, out, after)
    return out


def pack896(part):
    low = jnp.concatenate([part[:, 512:], jnp.zeros((8, 128), part.dtype)], axis=1)
    return jnp.concatenate([part[:, :512], low], axis=0)


def kernel(
    ql_hbm, qr_hbm, ck_hbm, cr_hbm, sl_hbm, sr_hbm, wuv_hbm, wo_hbm, wg_hbm, wu_hbm, wd_hbm,
    len_hbm, par_hbm, hid_hbm, gain_hbm, ids_hbm, gw_hbm,
    att_ref, upd_ref,
    hid_ref, gain_ref, ids_ref, gw_ref, rope, ropes, qc, qv0, qv1, kv, kr, s0, s1, sr0, sr1,
    wuv, wo, wg, wu, wd, tmp, st, ob, osb, br, bsr, zt, zsb, zss, zr, zrs,
    csb, cr1, c2, c3, c3o, res, nrm, e1f, esb, er1, e2b, er2,
    len_ref, par_ref, ss, rs, ls, here,
):
    ctx, hx = lax.axis_index("ctx"), lax.axis_index("hx")
    x, z = lax.div(ctx, 8), lax.rem(ctx, 8)
    y, k = lax.div(hx, 2), lax.rem(hx, 2)
    chip = ctx * 4 + y

    def dev(dx=0, dy=0, dz=0, dk=0):
        xx, yy = lax.rem(x + dx, 4), lax.rem(y + dy, 4)
        zz, kk = lax.rem(z + dz, 8), lax.rem(k + dk, 2)
        return (xx * 8 + zz, yy * 2 + kk)

    count = [0, 0]
    sends = []

    def remote(src, dst, where):
        i = count[0]
        count[0] += 1
        copy = pltpu.make_async_remote_copy(
            src_ref=src, dst_ref=dst, send_sem=ss.at[i], recv_sem=rs.at[i],
            device_id=where, device_id_type=MESH,
        )
        copy.start()
        sends.append(copy)
        return copy

    def flush():
        for copy in sends:
            copy.wait_send()
        sends.clear()

    def local(src, dst):
        i = count[1]
        count[1] += 1
        copy = pltpu.make_async_copy(src, dst, ls.at[i])
        copy.start()
        return copy

    kk = 1 - k
    head_rows = pl.ds(pl.multiple_of(hx * 16, 16), 16)
    key_rows = pl.ds(pl.multiple_of(k * 512, 512), 512)
    suf_rows = pl.ds(pl.multiple_of(k * 128, 128), 128)
    uo_rows = pl.ds(pl.multiple_of(k * 64, 64), 64)
    unit_rows = pl.ds(pl.multiple_of(k * 128, 128), 128)
    sv, srv = (s0, s1), (sr0, sr1)

    def kv_pairs(r, core):
        rows = slice(DR * r, DR * r + DR)
        return (
            (ck_hbm.at[2 * core + r], kv.at[r, key_rows]),
            (sl_hbm.at[pl.ds(8 * core + 4 * r, 4)], sv[r].at[:, suf_rows]),
            (cr_hbm.at[2 * core + r], kr.at[r, rows, key_rows]),
            (sr_hbm.at[pl.ds(8 * core + 4 * r, 4)], srv[r].at[:, rows, suf_rows]),
        )

    w_pairs = (
        (wuv_hbm, wuv.at[k]),
        (wo_hbm, wo.at[uo_rows]),
        (wg_hbm, wg.at[unit_rows]),
        (wu_hbm, wu.at[unit_rows]),
        (wd_hbm, wd.at[unit_rows]),
    )

    HX = [(dy, dk) for dy in (2, 1, 3, 0) for dk in range(2) if dy or dk]
    XY = [(dx, dy) for dx in range(4) for dy in range(4) if dx or dy]
    XY.sort(key=lambda d: -min(d[0], 4 - d[0]) - min(d[1], 4 - d[1]))
    ZK = [(dz, dk) for dz in (4, 3, 5, 2, 6, 1, 7, 0) for dk in range(2) if dz or dk]

    barrier = pltpu.get_barrier_semaphore()
    near = [dev(dx=1), dev(dx=3), dev(dz=1), dev(dz=7)]
    peers = [dev(dy=dy, dk=dk) for dy, dk in HX] + near
    for peer in peers:
        pl.semaphore_signal(barrier, inc=1, device_id=peer, device_id_type=MESH)
    own_q = [local(qr_hbm, rope)]
    own_q += [local(ql_hbm.at[pl.ds(8 * c, 4)], qc.at[c, :, :, :DL]) for c in range(2)]
    own = [[local(src, dst) for src, dst in kv_pairs(r, k)] for r in range(2)]
    own[0] += [local(len_hbm, len_ref), local(par_hbm, par_ref)]
    own[1].append(local(ql_hbm.at[pl.ds(8 * k + 4, 4)], qv1.at[:, head_rows]))
    own_w = [local(src, dst) for src, dst in w_pairs]
    small = [(hid_hbm, hid_ref), (gain_hbm, gain_ref), (ids_hbm, ids_ref), (gw_hbm, gw_ref)]
    own_small = [local(src, dst) for src, dst in small]
    kr[0, DR:] = jnp.zeros((DR, 1024), BF16)
    kr[1, :DR] = jnp.zeros((DR, 1024), BF16)
    sr0[:, DR:] = jnp.zeros((4, DR, 256), BF16)
    sr1[:, :DR] = jnp.zeros((4, DR, 256), BF16)
    own_q[0].wait()
    low = lax.broadcasted_iota(jnp.int32, (16, 128), 1) < DR
    for t in range(8):
        pair = rope[:, 128 * t : 128 * t + 128].astype(F32)
        swap = pltpu.roll(pair, DR, 1)
        ropes[pl.ds(2 * t, 16, stride=16), :] = jnp.where(low, pair, pltpu.roll(swap, 12, 0))
        ropes[pl.ds(2 * t + 1, 16, stride=16), :] = jnp.where(low, swap, pltpu.roll(pair, 12, 0))
    for c in range(2):
        for i in range(4):
            row = 16 * (8 * c + i)
            qc[c, i, :, DL:] = ropes[row : row + 16, :].astype(BF16)
    own_q[1].wait()
    own_q[2].wait()
    own[0].append(local(qc.at[k], qv0.at[:, head_rows]))
    pl.semaphore_wait(barrier, len(peers))

    def tell(i):
        for peer in near:
            pl.semaphore_signal(here.at[i], inc=1, device_id=peer, device_id_type=MESH)

    def hear(i):
        pl.semaphore_wait(here.at[i], len(near))

    beam = lax.rem(x + 2 * z, 4)
    got_q = {}
    for dy, dk in HX:
        core = lax.rem(k + dk, 2)
        if dy:
            src, dst = qc.at[core, beam], qv0.at[beam, head_rows]
        else:
            src, dst = qc.at[core], qv0.at[:, head_rows]
        got_q[dy, dk] = remote(src, dst, dev(dy=dy, dk=dk))
    tell(0)
    got_in = [[got_q[0, 1]], []]
    for src, dst in kv_pairs(0, kk):
        got_in[0].append(remote(src, dst, dev(dk=1)))
    for dy in (1, 3, 2):
        for copy in (got_q[dy, 0], got_q[dy, 1]):
            copy.wait_recv()
        rows = pl.ds(pl.multiple_of(lax.rem(y + 4 - dy, 4) * 32, 32), 32)
        block = qv0.at[beam, rows]
        for where in (dev(dx=1), dev(dx=3), dev(dz=1)):
            got_in[0].append(remote(block, block, where))

    hear(0)
    tell(1)
    for dy, dk in HX:
        core = lax.rem(k + dk, 2)
        src = ql_hbm.at[pl.ds(8 * core + 4, 4)]
        got_in[1].append(remote(src, qv1.at[:, head_rows], dev(dy=dy, dk=dk)))
    for src, dst in kv_pairs(1, kk):
        got_in[1].append(remote(src, dst, dev(dk=1)))
    def attend(r, beams):
        few = len(beams)
        first = beams[0]
        q = (qv1 if r else qv0)[first : first + few, :, :DL]
        qr = qv0[first : first + few, :, DL:]
        s = lax.dot_general(q.reshape(few * HEADS, DL), kv[r], NT, preferred_element_type=F32)
        s = s + jnp.dot(qr.reshape(few * HEADS, 128), kr[r], preferred_element_type=F32)
        pos = chip * 1024 + lax.broadcasted_iota(jnp.int32, (1, 1024), 1)
        s = jnp.where(pos < len_ref[2 * k + r], s * SCALE, NEG)
        high = jnp.max(s, axis=1, keepdims=True)
        rows = [slice(i * HEADS, (i + 1) * HEADS) for i in range(few)]
        own_s, tops, parent = [], [], []
        for i in range(few):
            p = lax.rem(par_ref[8 * k + 4 * r + first + i], 4)
            si = lax.dot_general(q[i], sv[r][p], NT, preferred_element_type=F32)
            si = si + jnp.dot(qr[i], srv[r][p], preferred_element_type=F32)
            own_s.append(si * SCALE)
            tops.append(jnp.maximum(high[rows[i]], jnp.max(own_s[i], axis=1, keepdims=True)))
            parent.append(p)
        w = jnp.exp2(s - jnp.concatenate(tops, axis=0)).astype(BF16)
        total = jnp.sum(w.astype(F32), axis=1, keepdims=True)
        acc = jnp.dot(w, kv[r], preferred_element_type=F32)
        totals = []
        for i in range(few):
            wi = jnp.exp2(own_s[i] - tops[i]).astype(BF16)
            totals.append(total[rows[i]] + jnp.sum(wi.astype(F32), axis=1, keepdims=True))
            ai = acc[rows[i]] + jnp.dot(wi, sv[r][parent[i]], preferred_element_type=F32)
            for l in range(4):
                tmp[i, l] = ai[:, 128 * l : 128 * l + 128]
        none = [0.0] * first
        rest = [0.0] * (4 - few - first)
        lane = lax.broadcasted_iota(jnp.int32, (HEADS, 128), 1)
        row = lax.broadcasted_iota(jnp.int32, (HEADS, 128), 0)
        lane = lane - 8 * jnp.bitwise_and(jnp.right_shift(row, 2), 7)
        stat = jnp.zeros((HEADS, 128), F32)
        for j, figure in enumerate(none + tops + rest + none + totals + rest):
            if not isinstance(figure, float):
                stat = jnp.where(lane == j, figure, stat)
        st[...] = st[...] + stat if first else stat
        for to in range(16):
            pick = pl.ds(32 * (to // 4) + to % 4, 8, stride=4)
            for l in range(4):
                block = jnp.concatenate([tmp[i, l, pick, :] for i in range(few)], axis=0)
                lanes = slice(128 * l, 128 * l + 128)
                ob[r, to, 8 * first : 8 * (first + few), lanes] = block.astype(BF16)
            if first + few == 4:
                osb[r, to] = jnp.sum(st[pick, :], axis=0, keepdims=True)

    me = x * 4 + y

    def join_send(r, beams):
        got = []
        rows = pl.ds(8 * beams[0], 8 * len(beams))
        for j, (dx, dy) in enumerate(XY):
            to = lax.rem(x + dx, 4) * 4 + lax.rem(y + dy, 4)
            if beams[-1] == 3:
                got.append(remote(osb.at[r, to], bsr.at[r, j], dev(dx=dx, dy=dy)))
            got.append(remote(ob.at[r, to, rows], br.at[r, j, rows], dev(dx=dx, dy=dy)))
        return got

    def join(r, got):
        for copy in got:
            copy.wait_recv()
        lane = lax.broadcasted_iota(jnp.int32, (8, 128), 1)
        lane = lane - 8 * lax.broadcasted_iota(jnp.int32, (8, 128), 0)

        def column(figures, j):
            return jnp.sum(jnp.where(lane == j, figures, 0.0), axis=1, keepdims=True)

        stats = [osb[r, me]] + [bsr[r, j] for j in range(15)]
        top = functools.reduce(jnp.maximum, stats)
        factors = [jnp.exp2(stat - top) for stat in stats]
        total = sum(pltpu.roll(f, 4, 1) * stat for f, stat in zip(factors, stats))
        for i in range(4):
            acc = jnp.zeros((8, DL), F32)
            for j in range(16):
                block = ob[r, me] if j == 0 else br[r, j - 1]
                rows = block.astype(F32)[8 * i : 8 * i + 8]
                acc = acc + rows * column(factors[j], i)
            at = pl.ds((4 * r + i) * 8, 8)
            for l in range(4):
                zt[l, at] = acc[:, 128 * l : 128 * l + 128]
            zt[4, at] = stat_lanes([column(top, i), column(total, 4 + i)], 8)

    hear(1)
    tell(2)
    for copy in own[0]:
        copy.wait()
    for copy in got_in[0]:
        copy.wait_recv()
    attend(0, [0, 1])
    got_b0 = join_send(0, [0, 1])
    attend(0, [2, 3])
    hear(2)
    tell(3)
    got_b0 += join_send(0, [2, 3])
    got_w = [remote(src, dst, dev(dk=1)) for src, dst in w_pairs]
    for copy in own[1]:
        copy.wait()
    for copy in got_in[1]:
        copy.wait_recv()
    attend(1, [0, 1, 2, 3])
    hear(3)
    got_b1 = join_send(1, [0, 1, 2, 3])
    join(0, got_b0)
    join(1, got_b1)
    for b in range(8):
        pick = pl.ds(b, 8, stride=8)
        for l in range(2):
            block = jnp.concatenate([zt[l, pick, :], zt[l + 2, pick, :]], axis=0)
            zsb[b, :, 128 * l : 128 * l + 128] = block.astype(BF16)
        zss[b] = zt[4, pick, :]
    got = []
    for dz in (4, 3, 5, 2, 6, 1, 7):
        to = lax.rem(z + dz, 8)
        got.append(remote(zss.at[to], zrs.at[dz - 1], dev(dz=dz)))
        got.append(remote(zsb.at[to], zr.at[dz - 1], dev(dz=dz)))
    for copy in got:
        copy.wait_recv()
    parts = []
    for a, t in [(zsb[z], zss[z])] + [(zr[j], zrs[j]) for j in range(7)]:
        a = a.astype(F32)
        parts.append((t[:, :1], t[:, 1:2], jnp.concatenate([a[:8], a[8:]], axis=1)))
    top, total, acc = fold(parts)
    attention = (acc / total).astype(BF16)

    for copy in own_w[:2]:
        copy.wait()
    for copy in got_w[:2]:
        copy.wait_recv()
    v0 = lax.dot_general(attention, wuv[0], NT, preferred_element_type=F32).astype(BF16)
    v1 = lax.dot_general(attention, wuv[1], NT, preferred_element_type=F32).astype(BF16)
    got = []
    for dz in (4, 3, 5, 2, 6, 1, 7, 0):
        b = lax.rem(z + dz, 8)
        cols = pl.ds(pl.multiple_of(b * 896, 128), 896)
        term = jnp.dot(v0, wo[:64, cols], preferred_element_type=F32)
        term = term + jnp.dot(v1, wo[64:, cols], preferred_element_type=F32)
        csb[b] = pack896(term).astype(BF16)
        if dz:
            got.append(remote(csb.at[b], cr1.at[dz - 1], dev(dz=dz)))
    flush()
    for copy in got:
        copy.wait_recv()
    part = csb[z].astype(F32)
    for j in range(7):
        part = part + cr1[j].astype(F32)
    c2[me] = part.astype(BF16)
    got = []
    for dx, dy in XY:
        got.append(remote(c2.at[me], c2.at[me], dev(dx=dx, dy=dy)))
    flush()
    for copy in got:
        copy.wait_recv()
    part = c2[0].astype(F32)
    for j in range(1, 16):
        part = part + c2[j].astype(F32)
    c3[z] = part.astype(BF16)
    got = []
    for dz in (4, 3, 5, 2, 6, 1, 7):
        got.append(remote(c3.at[z], c3.at[z], dev(dz=dz)))
    for copy in got:
        copy.wait_recv()
    got_att = remote(c3, c3o, dev(dk=1))

    for copy in own_small:
        copy.wait()
    square = jnp.zeros((8, 1), F32)
    for b in range(8):
        block = c3[b].astype(F32)
        for half, width in ((0, 512), (1, 384)):
            cols = slice(896 * b + 512 * half, 896 * b + 512 * half + width)
            hid = hid_ref[:, cols].astype(F32)
            hid = jnp.where(k == 0, hid[:8], hid[8:])
            value = hid + block[8 * half : 8 * half + 8, :width]
            res[:, cols] = value
            square = square + jnp.sum(value * value, axis=1, keepdims=True)
    scale = lax.rsqrt(square / D + 1e-6)
    nrm[...] = (res[...] * scale * gain_ref[...]).astype(BF16)

    expert = lax.div(ctx, 2)
    route = jnp.sum(gw_ref[...] * (ids_ref[...] == expert).astype(F32), axis=0, keepdims=True)
    row = lax.broadcasted_iota(jnp.int32, (8, HYPS), 0)
    col = lax.broadcasted_iota(jnp.int32, (8, HYPS), 1)
    route = jnp.sum(jnp.where(col == row + 8 * k, route, 0.0), axis=1, keepdims=True)
    for copy in own_w[2:]:
        copy.wait()
    for copy in got_w[2:]:
        copy.wait_recv()
    gate = lax.dot_general(nrm[...], wg[...], NT, preferred_element_type=F32)
    up = lax.dot_general(nrm[...], wu[...], NT, preferred_element_type=F32)
    act = (gate / (1.0 + jnp.exp(-gate)) * up * route).astype(BF16)
    start = x * 1792 + z * 224 + y * 56
    lane = lax.broadcasted_iota(jnp.int32, (8, 128), 1)
    got = []
    for dx in (2, 1, 3, 0):
        b = lax.rem(x + dx, 4)
        tiles = []
        for t in range(14):
            at = b * 1792 + 128 * t
            if t % 7 == 0:
                wide = pl.ds(pl.multiple_of(at, 128), 896)
                term = jnp.dot(act, wd[:, wide], preferred_element_type=F32)
            piece = term[:, 128 * (t % 7) : 128 * (t % 7) + 128]
            if dx == 0:
                col = lane + at
                mine = (col >= start) & (col < start + 56)
                rest = res[:, pl.ds(pl.multiple_of(at, 128), 128)]
                piece = piece + jnp.where(mine, rest, 0.0)
            tiles.append(piece)
        for c in range(4):
            halves = [
                jnp.where(
                    lane < 64,
                    window(tiles, 448 * u + 56 * c, 0),
                    window(tiles, 448 * u + 224 + 56 * c, 64),
                )
                for u in range(4)
            ]
            whole = jnp.concatenate(halves, axis=1)
            if dx == 0:
                e1f[c] = whole
            esb[4 * b + c] = jnp.concatenate([whole[:, :256], whole[:, 256:]], axis=0).astype(BF16)
        for dy in (2, 1, 3, 0):
            if dx or dy:
                to = 4 * b + lax.rem(y + dy, 4)
                got.append(remote(esb.at[to], er1.at[4 * dx + dy - 1], dev(dx=dx, dy=dy)))
    got_att.wait_recv()
    for b in range(8):
        a, o = c3[b].astype(F32), c3o[b].astype(F32)
        first, second = jnp.where(k == 0, a, o), jnp.where(k == 0, o, a)
        for half, width in ((0, 512), (1, 384)):
            cols = slice(896 * b + 512 * half, 896 * b + 512 * half + width)
            rows = slice(8 * half, 8 * half + 8)
            pair = jnp.concatenate([first[rows, :width], second[rows, :width]], axis=0)
            att_ref[:, cols] = pair.astype(BF16)
    flush()
    for copy in got:
        copy.wait_recv()
    part = er1[0].astype(F32)
    for j in range(1, 15):
        part = part + er1[j].astype(F32)
    part = jnp.concatenate([part[:8], part[8:]], axis=1) + e1f[y]
    for b in range(8):
        tile = part[:, 128 * (b // 2) : 128 * (b // 2) + 128]
        for c in range(2):
            off = 64 * (b % 2) + 28 * c
            e2b[2 * b + c] = pltpu.roll(tile, 128 - off, 1) if off else tile
    got = []
    for j, (dz, dk) in enumerate(ZK):
        to = lax.rem(z + dz, 8) * 2 + lax.rem(k + dk, 2)
        got.append(remote(e2b.at[to], er2.at[j], dev(dz=dz, dk=dk)))
    flush()
    for copy in got:
        copy.wait_recv()
    same, other = e2b[2 * z + k], jnp.zeros((8, 128), F32)
    for j, (dz, dk) in enumerate(ZK):
        if dk:
            other = other + er2[j]
        else:
            same = same + er2[j]
    both = jnp.concatenate(
        [jnp.where(k == 0, same, other), jnp.where(k == 0, other, same)], axis=0
    )
    upd_ref[...] = both[:, :28].astype(BF16)

    flush()


def local(
    query_latent, query_rope, cache_latent, cache_rope, suffix_latent, suffix_rope, lengths,
    parents, w_uv, w_o, hidden, norm_gain, w_gate, w_up, w_down, expert_ids, gate_weights,
):
    hbm = pl.BlockSpec(memory_space=pltpu.HBM)
    vmem = pl.BlockSpec(memory_space=pltpu.VMEM)
    scratch = [
        ((HYPS, D), BF16),
        ((1, D), F32),
        ((8, HYPS), jnp.int32),
        ((8, HYPS), F32),
        ((HYPS, 16 * DR), BF16),
        ((256, 128), F32),
        ((2, 4, 16, DL + 128), BF16),
        ((4, 128, DL + 128), BF16),
        ((4, 128, DL), BF16),
        ((2, 1024, DL), BF16),
        ((2, 2 * DR, 1024), BF16),
        ((4, 256, DL), BF16),
        ((4, 256, DL), BF16),
        ((4, 2 * DR, 256), BF16),
        ((4, 2 * DR, 256), BF16),
        ((2, 64, DL), BF16),
        ((128, D), BF16),
        ((256, D), BF16),
        ((256, D), BF16),
        ((256, D), BF16),
        ((4, 4, HEADS, 128), F32),
        ((HEADS, 128), F32),
        ((2, 16, 32, DL), BF16),
        ((2, 16, 1, 128), F32),
        ((2, 15, 32, DL), BF16),
        ((2, 15, 1, 128), F32),
        ((5, 64, 128), F32),
        ((8, 16, 256), BF16),
        ((8, 8, 128), F32),
        ((7, 16, 256), BF16),
        ((7, 8, 128), F32),
        ((8, 16, 512), BF16),
        ((7, 16, 512), BF16),
        ((16, 16, 512), BF16),
        ((8, 16, 512), BF16),
        ((8, 16, 512), BF16),
        ((8, D), F32),
        ((8, D), BF16),
        ((4, 8, 512), F32),
        ((16, 16, 256), BF16),
        ((15, 16, 256), BF16),
        ((16, 8, 128), F32),
        ((15, 8, 128), F32),
    ]
    return pl.pallas_call(
        kernel,
        name="decode_step",
        out_shape=(
            jax.ShapeDtypeStruct((HYPS, D), BF16),
            jax.ShapeDtypeStruct((HYPS, 28), BF16),
        ),
        in_specs=[hbm] * 17,
        out_specs=(vmem, vmem),
        scratch_shapes=[pltpu.VMEM(shape, dtype) for shape, dtype in scratch]
        + [
            pltpu.SMEM((4,), jnp.int32),
            pltpu.SMEM((16,), jnp.int32),
            pltpu.SemaphoreType.DMA((N_SEMS,)),
            pltpu.SemaphoreType.DMA((N_SEMS,)),
            pltpu.SemaphoreType.DMA((N_LOCAL,)),
            pltpu.SemaphoreType.REGULAR((4,)),
        ],
        compiler_params=pltpu.CompilerParams(
            collective_id=0, has_side_effects=True, vmem_limit_bytes=48 << 20
        ),
    )(
        *(
            pltpu.with_memory_space_constraint(value, pltpu.HBM)
            for value in (
                query_latent, query_rope, cache_latent, cache_rope, suffix_latent, suffix_rope,
                w_uv.T, w_o, w_gate, w_up, w_down, lengths, parents, hidden,
                norm_gain.reshape(1, D), expert_ids.T, gate_weights.T,
            )
        )
    )


def solution(mesh):
    both = ("ctx", "hx")
    in_specs = (
        P(None, "hx", None),
        P(None, "hx"),
        P(None, both, None),
        P(None, None, both),
        P(None, both, None),
        P(None, None, both),
        P(),
        P(),
        P(None, both),
        P(both, None),
        P(),
        P(),
        P(both, None),
        P(both, None),
        P(both, None),
        P(),
        P(),
    )
    out_specs = (P(), P(None, both))
    return jax.shard_map(local, mesh=mesh, in_specs=in_specs, out_specs=out_specs, check_vma=False)
```
